32 devices in a mesh: pipe: 2 (over x), expert: 16 (over z, y, core).
Axes of the slice: x: 2, y: 2, z: 4, core: 2. Of those that a mesh axis runs over, the one named last changes fastest.
Arguments:
- tokens: bfloat16 [2, 2048, 2560], P('pipe', 'expert'), may hold values from -48 to 48
- routes: int32 [2, 2048, 6], P('pipe', 'expert'), may hold values from 0 to 15, all different within a row; in each aligned block of 128 rows (0 to 127, 128 to 255, ..., all dimensions but the last counted through in order) at most 64 rows name the same one
- gates: float32 [2, 2048, 6], P('pipe', 'expert'), may hold values from 0.05 to 0.5
- capacity: int32 [2, 16], P('pipe'), may hold values from 32 to 64, as said below
- w_down_kv: bfloat16 [2, 2560, 256], P('pipe', 'expert'), may hold values from -1 to 1
- kv_gain: float32 [2, 256], P('pipe'), may hold values from 0.1 to 1.9
- w_query: bfloat16 [2, 256, 256], P('pipe'), may hold values from -1 to 12
- w_out: bfloat16 [2, 256, 2560], P('pipe', 'expert'), may hold values from -0.375 to 0.375
- w_gate_up: bfloat16 [2, 16, 2560, 1536], P('pipe', 'expert'), may hold values from -0.125 to 0.125
- w_expert_down: bfloat16 [2, 16, 768, 2560], P('pipe', 'expert'), may hold values from -0.21875 to 0.21875
Outputs:
- section_output: bfloat16 [2, 2048, 2560], P('pipe', 'expert')
The draws below stay inside these ranges and needn't reach their ends.
Inputs may be any that keep to these rules, and one draw needn't show every extreme that they name: `routes`: in each aligned block of 128 rows (the rows of one device) no expert is named by more than 64 rows of a micro-batch. `capacity`: in every section some expert accepts 64 rows.
All inputs are finite; a program needn't handle non-finite values.
Results may differ from the reference program's by a relative error of at most 0.019.
Values may be sent and summed in bfloat16 or wider, within the bound.
No kernel may reach another device: no remote copies, remote signals or barrier semaphores. Data moves between devices by JAX's collectives and lax.ppermute only.
A program may use at most 128 MiB of HBM per device.

```python
import math
import jax
import jax.numpy as jnp
import numpy as np
from jax import lax

D = 2560
KVL = 256
FE = 768
TOP = 6
TOK_DEV = 128
MICRO = 2
SEQ = 2048
EXPERTS = 16
MOST = 64
N_EXPERT = 16


def draw_tokens(key, part):
    own_key = jax.random.fold_in(key, 11)
    values = jnp.clip(jax.random.normal(own_key, (MICRO, SEQ, D), jnp.float32), -6.0, 6.0)
    return values.astype(jnp.bfloat16)


def draw_w_down_kv(key, part):
    own_key = jax.random.fold_in(key, 13)
    values = jnp.clip(jax.random.normal(own_key, (MICRO, D, KVL), jnp.float32), -6.0, 6.0) * D ** (-0.5)
    return values.astype(jnp.bfloat16)


def draw_kv_gain(key, part):
    own_key = jax.random.fold_in(key, 17)
    values = jax.random.uniform(own_key, (MICRO, KVL), jnp.float32, 0.1, 1.9)
    return values.astype(jnp.float32)


def draw_w_query(key, part):
    own_key = jax.random.fold_in(key, 19)
    values = jnp.clip(jax.random.normal(own_key, (MICRO, KVL, KVL), jnp.float32), -6.0, 6.0) * KVL ** (-0.5)
    return values.astype(jnp.bfloat16)


def draw_capacity(key, part):
    key = jax.random.fold_in(key, 7)
    first_key, second_key = jax.random.split(key)
    drawn = jax.random.randint(first_key, (MICRO, EXPERTS), max(1, MOST // 2), MOST + 1)
    chosen = jax.random.randint(second_key, (MICRO, 1), 0, EXPERTS)
    return jnp.where(jnp.arange(EXPERTS)[None, :] == chosen, MOST, drawn).astype(jnp.int32)


def block_scale(rng, extent, cuts, smallest, largest):
    def one(axis_at, parts):
        heights = jax.random.uniform(jax.random.fold_in(jax.random.fold_in(rng, 6), axis_at), (parts,), jnp.float32, smallest / len(cuts), largest / len(cuts))
        return jnp.repeat(jnp.exp(heights), extent[axis_at] // parts).reshape((-1,) + (1,) * (len(extent) - axis_at - 1))

    loudness = one(*cuts[0])
    for cut in cuts[1:]:
        loudness = loudness * one(*cut)
    return loudness


def assign_block(stream_key, own, number, rows, amount, top, bound, slope):
    order = jax.random.permutation(stream_key, amount)
    crowded, common = portions_of(amount, rows * top, bound, slope, True), portions_of(amount, rows * top, bound, slope, False)
    places = jnp.arange(amount)

    def named(lengths, offset_by):
        used = int((lengths > 0).sum())
        fixed = max(1, used // 4)
        moved = fixed + (places - fixed + offset_by * (used - fixed)) % max(1, amount - fixed)
        return jnp.zeros((amount,), jnp.int32).at[order[jnp.where(places < fixed, places, moved)]].set(jnp.asarray(lengths, jnp.int32))

    lengths = jnp.where(number % 4 == 0, named(crowded, number // 4), named(common, number - number // 4 - 1))
    mixed = jax.random.permutation(jax.random.fold_in(own, 3), amount)
    donor, sink = mixed[0:amount // 2 * 2:2], mixed[1:amount // 2 * 2:2]
    slack = jnp.minimum(lengths[donor] - 1, bound - lengths[sink]) // 2
    slack = jnp.where((donor == order[0]) | (sink == order[0]) | (lengths[sink] == 0), 0, jnp.maximum(slack, 0))
    moved = jax.random.randint(jax.random.fold_in(own, 4), (amount // 2,), 0, 1 << 20) % (slack + 1)
    lengths = lengths.at[donor].add(-moved).at[sink].add(moved)
    members = jnp.searchsorted(jnp.cumsum(lengths), jnp.arange(rows * top), side="right").astype(jnp.int32)
    table = members.reshape(top, rows).T
    table = table[jax.random.permutation(jax.random.fold_in(own, 1), rows)]
    offset_by = jax.random.randint(jax.random.fold_in(own, 2), (rows, 1), 0, top)
    return jnp.take_along_axis(table, (jnp.arange(top)[None, :] + offset_by) % top, axis=1)


def portions_of(count, total, most, skew, full):
    loads = [(1 << 20) // math.isqrt(grade ** skew) + 1 for grade in range(1, count + 1)]
    largest = most if full else min(most, max(-(-total // count), total * loads[0] // sum(loads)))
    least = 1 if total - largest >= count - 1 else 0
    holding, spare = [largest] + [least] * (count - 1), total - largest - least * (count - 1)
    while spare > 0:
        candidates = [i for i in range(1, count) if holding[i] < largest] or [i for i in range(1, count) if holding[i] < most]
        whole, left = sum([loads[i] for i in candidates]), spare
        for i in candidates:
            more = min(most - holding[i], max(1, left * loads[i] // whole), spare)
            holding[i] = holding[i] + more
            spare = spare - more
    return np.array(holding)


def gaussian(rng, dims, width, most, cuts=(), held_as=jnp.bfloat16):
    values = jax.random.normal(rng, dims, jnp.float32) * width
    if len(cuts) > 0:
        values = block_scale(rng, dims, cuts, -0.22, 0.18) * values
    return jnp.clip(values, min=-most, max=most).astype(held_as)


def setup_inputs(seed: int = 0) -> dict:
    seeds = jax.random.split(jax.random.key(seed), 11)
    tokens = draw_tokens(jax.random.fold_in(seeds[10], 71), 0)
    routes_keys = jax.random.split(jax.random.fold_in(seeds[1], 1), MICRO * SEQ // TOK_DEV)
    routes_turns = jax.random.permutation(jax.random.fold_in(seeds[1], 3), MICRO * SEQ // TOK_DEV)
    routes = jax.vmap(lambda own, number: assign_block(jax.random.fold_in(seeds[1], 2), own, number, TOK_DEV, EXPERTS, TOP, MOST, 2))(routes_keys, routes_turns).reshape((MICRO, SEQ, TOP))
    gates = jnp.clip(jnp.exp(math.log(0.5) - 2.3025851 * jax.random.uniform(seeds[2], (MICRO, SEQ, TOP), jnp.float32) ** block_scale(seeds[2], (MICRO, SEQ, TOP), ((0, 2), (1, 16)), -0.2, 0.2)), 0.05, 0.5)
    capacity = draw_capacity(jax.random.fold_in(seeds[10], 71), 0)
    w_down_kv = draw_w_down_kv(jax.random.fold_in(seeds[10], 71), 0)
    kv_gain = draw_kv_gain(jax.random.fold_in(seeds[10], 71), 0)
    w_query = draw_w_query(jax.random.fold_in(seeds[10], 71), 0)
    w_out = gaussian(seeds[7], (MICRO, KVL, D), KVL ** -0.5, 0.375, ((0, 2), (1, 16)))
    w_gate_up = gaussian(seeds[8], (MICRO, EXPERTS, D, 2 * FE), D ** -0.5, 0.125, ((0, 2), (1, 16)))
    w_expert_down = gaussian(seeds[9], (MICRO, EXPERTS, FE, D), FE ** -0.5, 0.21875, ((0, 2), (1, 16)))
    return {"tokens": tokens, "routes": routes, "gates": gates, "capacity": capacity, "w_down_kv": w_down_kv, "kv_gain": kv_gain, "w_query": w_query, "w_out": w_out, "w_gate_up": w_gate_up, "w_expert_down": w_expert_down}


def section_math(inputs, routes, gates, capacity, w_down_kv, kv_gain, w_query, w_out, w_gate_up, w_expert_down):
    raw = jnp.dot(inputs, w_down_kv, preferred_element_type=jnp.float32)
    latent = (raw * lax.rsqrt(lax.optimization_barrier(jnp.mean(raw * raw, -1, keepdims=True)) + 1e-06) * kv_gain).astype(jnp.bfloat16)
    query = jnp.dot(latent, w_query, preferred_element_type=jnp.float32).astype(jnp.bfloat16)
    scores = jnp.dot(query, latent.T, preferred_element_type=jnp.float32) * KVL ** (-0.5)
    places = jnp.arange(SEQ)
    causal = places[None, :] <= places[:, None]
    scores = jnp.where(causal, scores, -1e+30)
    peak = lax.optimization_barrier(jnp.max(scores, -1, keepdims=True))
    weights = jnp.where(causal, jnp.exp(scores - peak), 0.0)
    total = lax.optimization_barrier(jnp.sum(weights, -1, keepdims=True))
    accum = jnp.dot(weights.astype(jnp.bfloat16), latent, preferred_element_type=jnp.float32)
    attended = (accum / total).astype(jnp.bfloat16)
    hidden_state = (inputs.astype(jnp.float32) + jnp.dot(attended, w_out, preferred_element_type=jnp.float32)).astype(jnp.bfloat16)
    flat = routes.reshape(N_EXPERT, TOK_DEV * TOP)
    onehot = (flat[:, :, None] == jnp.arange(EXPERTS)[None, None, :]).astype(jnp.int32)
    ranking = lax.optimization_barrier(jnp.sum((jnp.cumsum(onehot, 1) - 1) * onehot, -1))
    limits = lax.optimization_barrier(jnp.sum(onehot * capacity[None, None, :], -1))
    kept = ranking < limits
    source = jnp.arange(N_EXPERT)[:, None]
    slots = EXPERTS * N_EXPERT * MOST
    target = jnp.where(kept, flat * (N_EXPERT * MOST) + source * MOST + ranking, slots).astype(jnp.int32)
    token_index = (source * TOK_DEV + jnp.arange(TOK_DEV * TOP)[None, :] // TOP).astype(jnp.int32)
    buffer = jnp.zeros((slots, D), hidden_state.dtype).at[target.reshape(-1)].set(hidden_state[token_index.reshape(-1)], mode='drop')

    def one_expert(packed):
        rows, gate_up, expert_down = packed
        both = jnp.dot(rows, gate_up, preferred_element_type=jnp.float32)
        inner = (jax.nn.silu(both[:, :FE]) * both[:, FE:]).astype(jnp.bfloat16)
        return jnp.dot(inner, expert_down, preferred_element_type=jnp.float32).astype(jnp.bfloat16)
    results = lax.map(one_expert, (buffer.reshape(EXPERTS, N_EXPERT * MOST, D), w_gate_up, w_expert_down))
    results = results.reshape(slots, D)
    picked = results[jnp.minimum(target, slots - 1).reshape(-1)]
    weight = jnp.where(kept.reshape(-1), gates.reshape(-1), 0.0)
    expert_sum = lax.optimization_barrier(jnp.sum((picked * weight[:, None]).reshape(SEQ, TOP, D), 1))
    return (hidden_state.astype(jnp.float32) + expert_sum).astype(jnp.bfloat16)

def reference(tokens, routes, gates, capacity, w_down_kv, kv_gain, w_query, w_out, w_gate_up, w_expert_down):
    outputs = lax.map(lambda packed: section_math(*packed), (tokens, routes, gates, capacity, w_down_kv, kv_gain, w_query, w_out, w_gate_up, w_expert_down))
    return jnp.roll(outputs, 1, axis=0)
```

```python
import functools

import jax
import jax.numpy as jnp
import numpy as np
from jax import lax
from jax.experimental import pallas as pl
from jax.experimental.pallas import tpu as pltpu
from jax.sharding import PartitionSpec as P

BF = jnp.bfloat16
F32 = jnp.float32
VMEM = pl.BlockSpec(memory_space=pltpu.VMEM)
SMEM = pl.BlockSpec(memory_space=pltpu.SMEM)
LIMIT = 48 * 1024 * 1024


def chip_at(place, chips):
    place %= chips
    half = chips // 2
    return 2 * place if place < half else 2 * (chips - 1 - place) + 1


def call(body, outs, ins, limit=LIMIT, flops=0, moved=0):
    return pl.pallas_call(
        body,
        out_shape=outs,
        in_specs=ins,
        out_specs=jax.tree.map(lambda _: VMEM, outs),
        compiler_params=pltpu.CompilerParams(vmem_limit_bytes=limit),
        cost_estimate=pl.CostEstimate(flops=flops, transcendentals=0, bytes_accessed=moved),
    )


def dot(a, b):
    return jnp.dot(a, b, preferred_element_type=F32)


def dot_first(a, b):
    return lax.dot_general(a, b, (((0,), (0,)), ((), ())), preferred_element_type=F32)


def dot_last(a, b):
    return lax.dot_general(a, b, (((1,), (1,)), ((), ())), preferred_element_type=F32)


def slots_of(row, most):
    ids = lax.broadcasted_iota(jnp.int32, (most, row.shape[1]), 0).astype(F32)
    return jnp.where(ids == row, 1.0, 0.0)


def pack_body(routes, gates, capacity, down, out, aux):
    rows, top = routes.shape
    experts = capacity.shape[1]
    width = out.shape[1]
    latent = down.shape[1]
    expert = lax.broadcasted_iota(jnp.int32, (rows, experts), 1)
    named = jnp.zeros((rows, experts), F32)
    gate = jnp.zeros((rows, experts), F32)
    for k in range(top):
        hit = routes[:, k : k + 1] == expert
        named = named + jnp.where(hit, 1.0, 0.0)
        gate = gate + jnp.where(hit, gates[:, k : k + 1], 0.0)
    row = lax.broadcasted_iota(jnp.int32, (rows, rows), 0)
    col = lax.broadcasted_iota(jnp.int32, (rows, rows), 1)
    rank = dot(jnp.where(row > col, 1.0, 0.0).astype(BF), named.astype(BF))
    kept = (named > 0.5) & (rank < capacity[...].astype(F32))
    same = jnp.where(row == col, 1.0, 0.0).astype(BF)
    slot = dot_first(jnp.where(kept, rank, -1.0).astype(BF), same)
    gate = dot_first(jnp.where(kept, gate, 0.0).astype(BF), same)
    aux[...] = jnp.zeros_like(aux)
    for q in range(down.shape[0] // 16):
        aux[0:16, q * latent : (q + 1) * latent] = down[16 * q : 16 * q + 16, :]
    aux[16:32, 0:width] = out[...]
    aux[0:experts, width : width + rows] = slot.astype(BF)
    aux[0:experts, width + rows : width + 2 * rows] = gate.astype(BF)


def unpack_body(groups, ids, aux, down, meta):
    owners, _, wide = aux.shape
    latent = down.shape[1]
    rows = meta.shape[1] // 2
    chips = owners // 2
    for e in range(owners):
        for q in range(groups):
            at = (e * groups + q) * 16
            down[at : at + 16, :] = aux[e, 0:16, q * latent : (q + 1) * latent]
    row = lax.broadcasted_iota(jnp.int32, (32, 2 * rows), 0)
    for part, (blocks, expert) in enumerate(((0, 0), (0, 1), (1, 0))):
        mine = row == ids[2, expert]
        for k in range(chips):
            block = aux[ids[blocks, k], :, wide - 2 * rows : wide].astype(F32)
            meta[part * chips + k : part * chips + k + 1, :] = jnp.sum(
                jnp.where(mine, block, 0.0), 0, keepdims=True
            )


def arrive_body(ks, most, chips, meta, down, gain, *refs):
    count = len(ks)
    pieces, (own, other, latents) = refs[: 2 * count], refs[2 * count :]
    for i, k in enumerate(ks):
        x = jnp.concatenate([pieces[2 * i][...], pieces[2 * i + 1][...]], 0)
        rows = x.shape[0]
        pick = jnp.concatenate(
            [slots_of(meta[j * chips + k : j * chips + k + 1, 0:rows], most) for j in (0, 1)], 0
        ).astype(BF)
        chosen = dot(pick, x).astype(BF)
        own[i] = chosen[:most]
        other[i] = chosen[most:]
        raw = dot(x, down[...])
        scale = lax.rsqrt(jnp.mean(raw * raw, -1, keepdims=True) + 1e-06)
        latents[i] = (raw * scale * gain[...]).astype(BF)


def attend(rows, place, keys, key_place, w_query):
    query = (dot(rows, w_query) * (rows.shape[1] ** -0.5)).astype(BF)
    scores = [
        jnp.where(at <= place, dot_last(query, piece), -1e30)
        for piece, at in zip(keys, key_place, strict=True)
    ]
    peak = functools.reduce(jnp.maximum, [jnp.max(s, -1, keepdims=True) for s in scores])
    weights = [jnp.exp(s - peak) for s in scores]
    total = sum(jnp.sum(w, -1, keepdims=True) for w in weights)
    accum = sum(dot(w.astype(BF), piece) for w, piece in zip(weights, keys, strict=True))
    return (accum / total).astype(BF)


def load_keys(latents, places):
    keys = [ref[...].reshape(-1, ref.shape[-1]) for ref in latents]
    spots, start = [], 0
    for key in keys:
        spots.append(places[:, start : start + key.shape[0]])
        start += key.shape[0]
    return keys, spots


def expert_body(ks, groups, most, chips, ids, meta, places, w_query, w_out, gate_up, expert_down, *refs):
    n = len(groups)
    own, other, lat_a, lat_b = (refs[i * n : (i + 1) * n] for i in range(4))
    out_a, out_b = refs[4 * n :]
    rows = lat_a[0].shape[1]
    hidden_width = expert_down.shape[0]
    keys, spots = load_keys(list(lat_a) + list(lat_b), places)
    where = {k: (g, i) for g, group in enumerate(groups) for i, k in enumerate(group)}
    chosen, latent, place, gate = [], [], [], []
    for side, (xs, lats) in enumerate(((own, lat_a), (other, lat_b))):
        for k in ks:
            g, i = where[k]
            at = (0 if side == 0 else 2 * chips) + k
            pick = slots_of(meta[at : at + 1, 0:rows], most)
            token = lax.broadcasted_iota(jnp.int32, (most, rows), 1).astype(F32)
            spot = jnp.sum(pick * token, -1, keepdims=True).astype(jnp.int32)
            place.append(spot + ids[side, k] * rows)
            gate.append(jnp.sum(pick * meta[at : at + 1, rows : 2 * rows], -1, keepdims=True))
            latent.append(dot(pick.astype(BF), lats[g][i]).astype(BF))
            chosen.append(xs[g][i])
    attended = attend(
        jnp.concatenate(latent, 0), jnp.concatenate(place, 0), keys, spots, w_query[...]
    )
    hidden = (jnp.concatenate(chosen, 0).astype(F32) + dot(attended, w_out[...])).astype(BF)
    both = dot(hidden, gate_up[...])
    inner = (jax.nn.silu(both[:, :hidden_width]) * both[:, hidden_width:]).astype(BF)
    result = (dot(inner, expert_down[...]) * jnp.concatenate(gate, 0)).astype(BF)
    half = len(ks) * most
    out_a[...] = result[:half]
    out_b[...] = result[half:]


def spread(k, most, chips, rows, meta, mine, theirs, cols):
    one = slots_of(meta[k : k + 1, 0:rows], most).astype(BF)
    two = slots_of(meta[chips + k : chips + k + 1, 0:rows], most).astype(BF)
    return dot_first(one, mine[:, cols]) + dot_first(two, theirs[:, cols])


def combine_body(k, at, most, chips, first, size, meta, mine, theirs, *refs):
    rows = meta.shape[1] // 2
    cols = slice(first, first + size)
    spot = slice(at * most, (at + 1) * most)
    total = spread(k, most, chips, rows, meta, mine.at[spot], theirs.at[spot], cols)
    if len(refs) > 1:
        total = total + refs[0][...].astype(F32)
    refs[-1][...] = total.astype(BF)


def own_body(at, most, chips, n, ids, meta, places, w_query, w_out, tokens, mine, theirs, *refs):
    latents, outs = refs[: 2 * n], refs[2 * n :]
    rows = tokens.shape[0]
    keys, spots = load_keys(latents, places)
    place = ids[0, 0] * rows + lax.broadcasted_iota(jnp.int32, (rows, 1), 0)
    attended = attend(latents[0][0], place, keys, spots, w_query[...])
    hidden = (tokens[...].astype(F32) + dot(attended, w_out[...])).astype(BF).astype(F32)
    spot = slice(at * most, (at + 1) * most)
    first = 0
    for out in outs:
        cols = slice(first, first + out.shape[1])
        total = spread(0, most, chips, rows, meta, mine.at[spot], theirs.at[spot], cols)
        out[...] = (hidden[:, cols] + total).astype(BF)
        first += out.shape[1]


def final_body(*refs):
    ins, out = refs[:-1], refs[-1]
    first = 0
    for one, two in zip(ins[0::2], ins[1::2], strict=True):
        size = one.shape[1]
        out[:, first : first + size] = (one[...].astype(F32) + two[...].astype(F32)).astype(BF)
        first += size


def on_device(
    tokens, routes, gates, capacity, w_down_kv, kv_gain, w_query, w_out, w_gate_up, w_expert_down
):
    pipes = lax.axis_size("pipe")
    owners = lax.axis_size("expert")
    chips = owners // 2
    me = lax.axis_index("expert")
    rows, width = tokens.shape[1:]
    top = routes.shape[2]
    latent = w_query.shape[1]
    most = max(2, 4 * rows * top // (3 * owners))
    shape = jax.ShapeDtypeStruct

    ring, blocks = [], np.zeros((owners, chips), np.int32)
    for r in range(chips):
        even, odd = 2 * chip_at(r, chips), 2 * chip_at(r, chips) + 1
        ring.append((even, 2 * chip_at(r + 1, chips)))
        ring.append((odd, 2 * chip_at(r - 1, chips) + 1))
        for k in range(chips):
            blocks[even, k] = 2 * chip_at(r - k, chips)
            blocks[odd, k] = 2 * chip_at(r + k, chips) + 1
    step = lambda x: lax.ppermute(x, "expert", ring)
    sibling = lambda x: lax.ppermute(x, "expert", [(i, i ^ 1) for i in range(owners)])
    last = [
        (p * owners + a, ((p + 1) % pipes) * owners + b) for p in range(pipes) for a, b in ring
    ]
    onward = lambda x: lax.ppermute(x, "pipe", [(p, (p + 1) % pipes) for p in range(pipes)])

    table = jnp.asarray(np.stack([blocks, blocks[np.arange(owners) ^ 1]], 1))
    order = lax.dynamic_index_in_dim(table, me, 0, keepdims=False)
    whose = jnp.zeros((chips,), jnp.int32).at[0].set(me).at[1].set(me ^ 1)
    ids = jnp.concatenate([order, whose[None]], 0)
    places = (order[:, :, None] * rows + jnp.arange(rows)[None, None, :]).reshape(1, -1)

    out_shard = w_out[0]
    if out_shard.shape[0] < 16:
        out_shard = jnp.pad(out_shard, ((0, 16 - out_shard.shape[0]), (0, 0)))
    aux = call(pack_body, shape((32, width + 2 * rows), BF), [VMEM] * 5)(
        routes[0], gates[0], capacity, w_down_kv[0], out_shard
    )
    aux = lax.all_gather(aux, "expert", axis=0)
    down, meta = call(
        functools.partial(unpack_body, w_down_kv.shape[1] // 16),
        (shape((owners * w_down_kv.shape[1], latent), BF), shape((3 * chips, 2 * rows), F32)),
        [SMEM, VMEM],
    )(ids, aux)
    out_proj = aux[:, 16 : 16 + w_out.shape[1], :width].reshape(-1, width)

    half = rows // 2
    held = [(tokens[0, :half], tokens[0, half:])]
    for k in range(1, chips):
        held.append(tuple(step(x) for x in held[-1]))

    cut = chips - 2
    groups = (tuple(range(cut)), tuple(range(cut, chips)))
    own, other, lat_a, lat_b = [], [], [], []
    for group in groups:
        n = len(group)
        picked, away, lat = call(
            functools.partial(arrive_body, group, most, chips),
            (
                shape((n, most, width), BF),
                shape((n, most, width), BF),
                shape((n, rows, latent), BF),
            ),
            [VMEM] * (3 + 2 * n),
            flops=2 * n * rows * width * (latent + 2 * most),
        )(meta, down, kv_gain, *[x for k in group for x in held[k]])
        own.append(picked)
        other.append(sibling(away))
        lat_a.append(lat)
        lat_b.append(sibling(lat))

    sequence = list(range(1, chips)) + [0]
    chunks = [sequence[i : i + 2] for i in range(0, chips, 2)]
    gate_up, expert_down = w_gate_up[0, 0], w_expert_down[0, 0]
    mine, theirs = {}, {}
    for ks in chunks:
        size = len(ks) * most
        out_a, out_b = call(
            functools.partial(expert_body, tuple(ks), groups, most, chips),
            (shape((size, width), BF), shape((size, width), BF)),
            [SMEM] + [VMEM] * (6 + 4 * len(groups)),
            flops=4 * size * (3 * width * expert_down.shape[0] + 2 * latent * owners * rows),
        )(
            ids,
            meta,
            places,
            w_query[0],
            out_proj,
            gate_up,
            expert_down,
            *own,
            *other,
            *lat_a,
            *lat_b,
        )
        back = sibling(out_b)
        for i, k in enumerate(ks):
            mine[k], theirs[k] = (out_a, i), (back, i)

    pieces = [(0, width // 2), (width // 2, width - width // 2)]
    passing = [None] * len(pieces)
    for k in range(1, chips):
        for i, (first, size) in enumerate(pieces):
            more = [] if passing[i] is None else [passing[i]]
            total = call(
                functools.partial(combine_body, k, mine[k][1], most, chips, first, size),
                shape((rows, size), BF),
                [VMEM] * (3 + len(more)),
                flops=4 * rows * most * size,
            )(meta, mine[k][0], theirs[k][0], *more)
            if k < chips - 1:
                passing[i] = step(total)
            else:
                passing[i] = lax.ppermute(total, ("pipe", "expert"), last)
    kept = call(
        functools.partial(own_body, mine[0][1], most, chips, len(groups)),
        tuple(shape((rows, size), BF) for _, size in pieces),
        [SMEM] + [VMEM] * (7 + 2 * len(groups)),
        flops=2 * rows * latent * (width + 2 * owners * rows),
    )(ids, meta, places, w_query[0], out_proj, tokens[0], mine[0][0], theirs[0][0], *lat_a, *lat_b)
    kept = [onward(x) for x in kept]
    output = call(final_body, shape((rows, width), BF), [VMEM] * (2 * len(pieces)))(
        *[x for pair in zip(kept, passing, strict=True) for x in pair]
    )
    return output[None]


def solution(mesh):
    return jax.shard_map(
        on_device,
        mesh=mesh,
        in_specs=(
            P("pipe", "expert", None),
            P("pipe", "expert", None),
            P("pipe", "expert", None),
            P("pipe", None),
            P("pipe", "expert", None),
            P("pipe", None),
            P("pipe", None, None),
            P("pipe", "expert", None),
            P("pipe", "expert", None, None),
            P("pipe", "expert", None, None),
        ),
        out_specs=P("pipe", "expert", None),
        check_vma=False,
    )
```

```python
import functools

import jax
import jax.numpy as jnp
import numpy as np
from jax import lax
from jax.experimental import pallas as pl
from jax.experimental.pallas import tpu as pltpu
from jax.sharding import PartitionSpec as P

BF = jnp.bfloat16
F32 = jnp.float32
VMEM = pl.BlockSpec(memory_space=pltpu.VMEM)
SMEM = pl.BlockSpec(memory_space=pltpu.SMEM)
MIB = 1024 * 1024


def chip_at(place, chips):
    place %= chips
    half = chips // 2
    return 2 * place if place < half else 2 * (chips - 1 - place) + 1


def call(body, outs, ins, limit=12, flops=0, moved=0):
    return pl.pallas_call(
        body,
        out_shape=outs,
        in_specs=ins,
        out_specs=jax.tree.map(lambda _: VMEM, outs),
        compiler_params=pltpu.CompilerParams(vmem_limit_bytes=limit * MIB),
        cost_estimate=pl.CostEstimate(flops=flops, transcendentals=0, bytes_accessed=moved),
    )


def dot(a, b):
    return jnp.dot(a, b, preferred_element_type=F32)


def dot_first(a, b):
    return lax.dot_general(a, b, (((0,), (0,)), ((), ())), preferred_element_type=F32)


def dot_last(a, b):
    return lax.dot_general(a, b, (((1,), (1,)), ((), ())), preferred_element_type=F32)


def slots_of(row, most):
    ids = lax.broadcasted_iota(jnp.int32, (most, row.shape[1]), 0).astype(F32)
    return jnp.where(ids == row, 1.0, 0.0)


def pack_body(routes, gates, capacity, down, out):
    top, _, rows = routes.shape
    experts = capacity.shape[1]
    expert = lax.broadcasted_iota(jnp.int32, (experts, rows), 0)
    named = jnp.zeros((experts, rows), F32)
    gate = jnp.zeros((experts, rows), F32)
    for k in range(top):
        hit = routes[k] == expert
        named = named + jnp.where(hit, 1.0, 0.0)
        gate = gate + jnp.where(hit, gates[k], 0.0)
    row = lax.broadcasted_iota(jnp.int32, (rows, rows), 0)
    col = lax.broadcasted_iota(jnp.int32, (rows, rows), 1)
    rank = dot(named.astype(BF), jnp.where(row < col, 1.0, 0.0).astype(BF))
    row = lax.broadcasted_iota(jnp.int32, (experts, experts), 0)
    col = lax.broadcasted_iota(jnp.int32, (experts, experts), 1)
    limit = jnp.sum(jnp.where(row == col, capacity[...].astype(F32), 0.0), 1, keepdims=True)
    kept = (named > 0.5) & (rank < limit)
    depth = down.shape[0]
    out[0:depth, :] = down[...]
    out[depth : depth + experts, 0:rows] = jnp.where(kept, rank, -1.0).astype(BF)
    out[depth : depth + experts, rows : 2 * rows] = jnp.where(kept, gate, 0.0).astype(BF)


def unpack_body(depth, ids, one, two, down, meta):
    chips, tall, wide = one.shape
    experts = tall - depth
    row = lax.broadcasted_iota(jnp.int32, (experts, wide), 0)
    for side, half in enumerate((one, two)):
        for k in range(chips):
            block = ids[side, k]
            down[pl.ds(pl.multiple_of(block * depth, 16), depth), :] = half[k, 0:depth, :]
            table = half[k, depth:tall, :].astype(F32)
            own = jnp.sum(jnp.where(row == ids[2, 0], table, 0.0), 0, keepdims=True)
            meta[side * chips + k : side * chips + k + 1, :] = own
            meta[pl.ds(3 * chips + block, 1), :] = own
            if side == 0:
                meta[2 * chips + k : 2 * chips + k + 1, :] = jnp.sum(
                    jnp.where(row == ids[2, 1], table, 0.0), 0, keepdims=True
                )


def arrive_body(ks, most, chips, meta, down, gain, *refs):
    count = len(ks)
    pieces, (own, other, latents) = refs[: 2 * count], refs[2 * count :]
    rows = latents.shape[1]
    half = rows // 2
    for i, k in enumerate(ks):
        x = jnp.concatenate([pieces[2 * i][...], pieces[2 * i + 1][0:half, :]], 0)
        pick = jnp.concatenate(
            [slots_of(meta[at : at + 1, 0:rows], most) for at in (k, 2 * chips + k)], 0
        ).astype(BF)
        chosen = dot(pick, x).astype(BF)
        own[i] = chosen[:most]
        other[i] = chosen[most:]
        raw = dot(x, down[...])
        scale = lax.rsqrt(jnp.mean(raw * raw, -1, keepdims=True) + 1e-06)
        latents[i] = (raw * scale * gain[...]).astype(BF)


def attend(rows, keys, masks, w_query):
    query = (dot(rows, w_query) * (rows.shape[1] ** -0.5)).astype(BF)
    scores = [dot_last(query, piece) for piece in keys]
    scores = [s if m is None else jnp.where(m, s, -1e30) for s, m in zip(scores, masks, strict=True)]
    peak = functools.reduce(jnp.maximum, [jnp.max(s, -1, keepdims=True) for s in scores])
    weights = [jnp.exp(s - peak) for s in scores]
    total = sum(jnp.sum(w, -1, keepdims=True) for w in weights)
    accum = sum(dot(w.astype(BF), piece) for w, piece in zip(weights, keys, strict=True))
    return (accum / total).astype(BF)


def reorder(attended, order):
    place = lax.broadcasted_iota(jnp.int32, (attended.shape[1], order.shape[1]), 0)
    return dot(attended, jnp.where(place == order, 1.0, 0.0).astype(BF)).astype(BF)


def expert_body(groups, most, chips, sequence, early, ids, order, meta, w_query, out_a, out_b, *refs):
    n = len(groups)
    gate_up_hbm, expert_down_hbm = refs[:2]
    own, other, lat_a, lat_b = (refs[2 + i * n : 2 + (i + 1) * n] for i in range(4))
    mine, theirs_early, theirs_late, lat, gate_up, expert_down, att, sem = refs[2 + 4 * n :]
    loads = [
        pltpu.make_async_copy(gate_up_hbm, gate_up, sem.at[0]),
        pltpu.make_async_copy(expert_down_hbm, expert_down, sem.at[1]),
    ]
    for load in loads:
        load.start()
    rows = lat_a[0].shape[1]
    hidden_width = expert_down.shape[0]
    blocks = 2 * chips
    where = {k: (g, i) for g, group in enumerate(groups) for i, k in enumerate(group)}
    for side, halves in enumerate((lat_a, lat_b)):
        for k in range(chips):
            g, i = where[k]
            lat[pl.ds(pl.multiple_of(ids[side, k] * rows, rows), rows), :] = halves[g][i]
    batch = 4
    token = lax.broadcasted_iota(jnp.int32, (most, rows), 1).astype(F32)
    for first in range(0, blocks, batch):
        latent, place = [], []
        for b in range(first, first + batch):
            pick = slots_of(meta[3 * chips + b : 3 * chips + b + 1, 0:rows], most)
            spot = jnp.sum(pick * token, -1, keepdims=True).astype(jnp.int32)
            place.append(spot + (b - first) * rows)
            latent.append(dot(pick.astype(BF), lat[b * rows : (b + 1) * rows, :]).astype(BF))
        place = jnp.concatenate(place, 0)
        key = lax.broadcasted_iota(jnp.int32, (1, batch * rows), 1)
        keys, masks = [lat[first * rows : (first + batch) * rows, :]], [key <= place]
        if first:
            keys.append(lat[0 : first * rows, :])
            masks.append(None)
        attended = attend(jnp.concatenate(latent, 0), keys, masks, w_query[...])
        attended = reorder(attended, order[...])
        for b in range(first, first + batch):
            at = pl.multiple_of(ids[3, b] * most, most)
            att[pl.ds(at, most), :] = attended[(b - first) * most : (b - first + 1) * most, :]
    for load in loads:
        load.wait()
    shard = out_a.shape[0]
    for ks in (sequence[: chips // 2], sequence[chips // 2 :]):
        chosen, attended, gate = [], [], []
        for side, xs in enumerate((own, other)):
            for k in ks:
                g, i = where[k]
                at = side * chips + k
                pick = slots_of(meta[at : at + 1, 0:rows], most)
                gate.append(jnp.sum(pick * meta[at : at + 1, rows : 2 * rows], -1, keepdims=True))
                attended.append(att[at * most : (at + 1) * most, :])
                chosen.append(xs[g][i])
        attended = jnp.concatenate(attended, 0)
        hidden = dot(attended[:, :shard], out_a[...]) + dot(attended[:, shard:], out_b[...])
        hidden = (jnp.concatenate(chosen, 0).astype(F32) + hidden).astype(BF)
        both = dot(hidden, gate_up[...])
        inner = (jax.nn.silu(both[:, :hidden_width]) * both[:, hidden_width:]).astype(BF)
        result = (dot(inner, expert_down[...]) * jnp.concatenate(gate, 0)).astype(BF)
        for i, k in enumerate(ks):
            mine[k] = result[i * most : (i + 1) * most]
            away = result[(len(ks) + i) * most : (len(ks) + i + 1) * most]
            if k in early:
                theirs_early[early.index(k)] = away
            else:
                theirs_late[[j for j in sequence if j not in early].index(k)] = away


def spread(k, most, chips, rows, meta, mine, theirs, cols):
    one = slots_of(meta[k : k + 1, 0:rows], most).astype(BF)
    two = slots_of(meta[2 * chips + k : 2 * chips + k + 1, 0:rows], most).astype(BF)
    return dot_first(one, mine[k, :, cols]) + dot_first(two, theirs[:, cols])


def combine_body(k, at, most, chips, first, size, meta, mine, theirs, *refs):
    rows = meta.shape[1] // 2
    total = spread(k, most, chips, rows, meta, mine, theirs.at[at], slice(first, first + size))
    if len(refs) > 1:
        total = total + refs[0][...].astype(F32)
    refs[-1][...] = total.astype(BF)


def own_body(at, most, chips, ids, order, meta, w_query, out_a, out_b, tokens, lat, mine, theirs, *outs):
    rows = tokens.shape[0]
    start = pl.multiple_of(ids[0, 0] * rows, rows)
    place = start + lax.broadcasted_iota(jnp.int32, (rows, 1), 0)
    key = lax.broadcasted_iota(jnp.int32, (1, lat.shape[0]), 1)
    attended = attend(lat[pl.ds(start, rows), :], [lat[...]], [key <= place], w_query[...])
    attended = reorder(attended, order[...])
    shard = out_a.shape[0]
    hidden = dot(attended[:, :shard], out_a[...]) + dot(attended[:, shard:], out_b[...])
    hidden = (tokens[...].astype(F32) + hidden).astype(BF).astype(F32)
    first = 0
    for out in outs:
        cols = slice(first, first + out.shape[1])
        total = spread(0, most, chips, rows, meta, mine, theirs.at[at], cols)
        out[...] = (hidden[:, cols] + total).astype(BF)
        first += out.shape[1]


def final_body(*refs):
    ins, out = refs[:-1], refs[-1]
    first = 0
    for one, two in zip(ins[0::2], ins[1::2], strict=True):
        size = one.shape[1]
        out[:, first : first + size] = (one[...].astype(F32) + two[...].astype(F32)).astype(BF)
        first += size


def after(x, *others):
    return lax.optimization_barrier((x, *others))[0]


def on_device(
    tokens, routes, gates, capacity, w_down_kv, kv_gain, w_query, w_out, w_gate_up, w_expert_down
):
    pipes = lax.axis_size("pipe")
    owners = lax.axis_size("expert")
    chips = owners // 2
    me = lax.axis_index("expert")
    rows, width = tokens.shape[1:]
    top = routes.shape[2]
    latent = w_query.shape[1]
    depth = w_down_kv.shape[1]
    most = max(2, 4 * rows * top // (3 * owners))
    shape = jax.ShapeDtypeStruct

    ring, blocks = [], np.zeros((owners, chips), np.int32)
    for r in range(chips):
        even, odd = 2 * chip_at(r, chips), 2 * chip_at(r, chips) + 1
        ring.append((even, 2 * chip_at(r + 1, chips)))
        ring.append((odd, 2 * chip_at(r - 1, chips) + 1))
        for k in range(chips):
            blocks[even, k] = 2 * chip_at(r - k, chips)
            blocks[odd, k] = 2 * chip_at(r + k, chips) + 1
    step = lambda x: lax.ppermute(x, "expert", ring)
    sibling = lambda x: lax.ppermute(x, "expert", [(i, i ^ 1) for i in range(owners)])
    last = [
        (p * owners + a, ((p + 1) % pipes) * owners + b) for p in range(pipes) for a, b in ring
    ]
    onward = lambda x: lax.ppermute(x, "pipe", [(p, (p + 1) % pipes) for p in range(pipes)])

    table = np.zeros((owners, 4, owners), np.int32)
    for e in range(owners):
        both = np.concatenate([blocks[e], blocks[e ^ 1]])
        table[e, 0, :chips], table[e, 1, :chips] = blocks[e], blocks[e ^ 1]
        table[e, 2, :2] = (e, e ^ 1)
        table[e, 3, both] = np.arange(owners)
    ids = lax.dynamic_index_in_dim(jnp.asarray(table), me, 0, keepdims=False)
    shard = w_out.shape[1]
    order = (ids[:2, :chips].reshape(-1)[:, None] * shard + jnp.arange(shard)[None, :]).reshape(1, -1)

    half = rows // 2
    first = [tokens[0, :half]]
    second = [jnp.concatenate([tokens[0, half:], w_out[0]], 0)]
    small = [
        call(pack_body, shape((depth + owners, latent), BF), [VMEM] * 4)(
            routes.transpose(2, 0, 1),
            gates.transpose(2, 0, 1),
            capacity,
            after(w_down_kv[0], first[0], second[0]),
        )
    ]
    arrived = []
    for _ in range(1, chips):
        for stream in (first, small, second, small):
            if len(stream) < chips:
                arrived.append(stream[-1])
                stream.append(step(after(stream[-1], *arrived[-3:-1])))
    small = jnp.stack(small)
    down, meta = call(
        functools.partial(unpack_body, depth),
        (shape((owners * depth, latent), BF), shape((5 * chips, 2 * rows), F32)),
        [SMEM, VMEM, VMEM],
    )(ids, small, sibling(small))

    groups = (tuple(range(chips - 3)), (chips - 3, chips - 2), (chips - 1,))
    own, other, lat_a, lat_b = [], [], [], []
    for group in groups:
        n = len(group)
        picked, away, lat = call(
            functools.partial(arrive_body, group, most, chips),
            (
                shape((n, most, width), BF),
                shape((n, most, width), BF),
                shape((n, rows, latent), BF),
            ),
            [VMEM] * (3 + 2 * n),
            flops=2 * n * rows * width * (latent + 2 * most),
        )(meta, down, kv_gain, *[x for k in group for x in (first[k], second[k])])
        own.append(picked)
        other.append(sibling(away))
        lat_a.append(lat)
        lat_b.append(sibling(lat))
    out_a = jnp.concatenate([x[half:] for x in second], 0)
    out_b = sibling(out_a)

    sequence = tuple(range(1, chips)) + (0,)
    early = sequence[:2]
    gate_up, expert_down = w_gate_up[0, 0], w_expert_down[0, 0]
    mine, away_early, away_late, lat = pl.pallas_call(
        functools.partial(expert_body, groups, most, chips, sequence, early),
        out_shape=(
            shape((chips, most, width), BF),
            shape((len(early), most, width), BF),
            shape((chips - len(early), most, width), BF),
            shape((owners * rows, latent), BF),
        ),
        in_specs=[SMEM] + [VMEM] * 5 + [pl.BlockSpec(memory_space=pl.ANY)] * 2 + [VMEM] * (4 * len(groups)),
        out_specs=(VMEM,) * 4,
        scratch_shapes=[
            pltpu.VMEM(gate_up.shape, BF),
            pltpu.VMEM(expert_down.shape, BF),
            pltpu.VMEM((owners * most, latent), BF),
            pltpu.SemaphoreType.DMA((2,)),
        ],
        compiler_params=pltpu.CompilerParams(vmem_limit_bytes=40 * MIB),
    )(
        ids,
        order,
        meta,
        w_query[0],
        out_a,
        out_b,
        gate_up,
        expert_down,
        *own,
        *other,
        *lat_a,
        *lat_b,
    )
    theirs_early, theirs_late = sibling(away_early), sibling(away_late)
    theirs = {}
    for i, k in enumerate(sequence):
        theirs[k] = (theirs_early, i) if i < len(early) else (theirs_late, i - len(early))

    pieces = [(0, width // 2), (width // 2, width - width // 2)]
    passing = [None] * len(pieces)
    for k in range(1, chips):
        if k == min(3, chips - 1):
            kept = call(
                functools.partial(own_body, theirs[0][1], most, chips),
                tuple(shape((rows, size), BF) for _, size in pieces),
                [SMEM] + [VMEM] * 9,
                flops=2 * rows * latent * (width + 2 * owners * rows),
            )(
                ids,
                order,
                meta,
                w_query[0],
                out_a,
                out_b,
                after(tokens[0], *passing),
                lat,
                mine,
                theirs[0][0],
            )
            passing = [after(x, *kept) for x in passing]
            kept = [onward(x) for x in kept]
        for i, (start, size) in enumerate(pieces):
            more = [] if passing[i] is None else [passing[i]]
            if k == chips - 2 and more:
                more = [after(more[0], *kept)]
            total = call(
                functools.partial(combine_body, k, theirs[k][1], most, chips, start, size),
                shape((rows, size), BF),
                [VMEM] * (3 + len(more)),
                flops=4 * rows * most * size,
            )(meta, mine, theirs[k][0], *more)
            if k < chips - 1:
                passing[i] = step(total)
            else:
                passing[i] = lax.ppermute(total, ("pipe", "expert"), last)
    output = call(final_body, shape((rows, width), BF), [VMEM] * (2 * len(pieces)))(
        *[x for pair in zip(kept, passing, strict=True) for x in pair]
    )
    return output[None]


def solution(mesh):
    return jax.shard_map(
        on_device,
        mesh=mesh,
        in_specs=(
            P("pipe", "expert", None),
            P("pipe", "expert", None),
            P("pipe", "expert", None),
            P("pipe", None),
            P("pipe", "expert", None),
            P("pipe", None),
            P("pipe", None, None),
            P("pipe", "expert", None),
            P("pipe", "expert", None, None),
            P("pipe", "expert", None, None),
        ),
        out_specs=P("pipe", "expert", None),
        check_vma=False,
    )
```

```python
import functools

import jax
import jax.numpy as jnp
import numpy as np
from jax import lax
from jax.experimental import pallas as pl
from jax.experimental.pallas import tpu as pltpu
from jax.sharding import PartitionSpec as P

BF = jnp.bfloat16
F32 = jnp.float32
VMEM = pl.BlockSpec(memory_space=pltpu.VMEM)
SMEM = pl.BlockSpec(memory_space=pltpu.SMEM)
MIB = 1024 * 1024
LONG = 10**11


def chip_at(place, chips):
    place %= chips
    half = chips // 2
    return 2 * place if place < half else 2 * (chips - 1 - place) + 1


def call(body, outs, ins, limit=12, flops=0):
    return pl.pallas_call(
        body,
        out_shape=outs,
        in_specs=ins,
        out_specs=jax.tree.map(lambda _: VMEM, outs),
        compiler_params=pltpu.CompilerParams(vmem_limit_bytes=limit * MIB),
        cost_estimate=pl.CostEstimate(flops=flops, transcendentals=0, bytes_accessed=flops // 100),
    )


def dot(a, b):
    return jnp.dot(a, b, preferred_element_type=F32)


def dot_first(a, b):
    return lax.dot_general(a, b, (((0,), (0,)), ((), ())), preferred_element_type=F32)


def dot_last(a, b):
    return lax.dot_general(a, b, (((1,), (1,)), ((), ())), preferred_element_type=F32)


def slots_of(row, most):
    ids = lax.broadcasted_iota(jnp.int32, (most, row.shape[1]), 0).astype(F32)
    return jnp.where(ids == row, 1.0, 0.0)


def pack_body(routes, gates, capacity, down, out):
    top, _, rows = routes.shape
    experts = capacity.shape[1]
    expert = lax.broadcasted_iota(jnp.int32, (experts, rows), 0)
    named = jnp.zeros((experts, rows), F32)
    gate = jnp.zeros((experts, rows), F32)
    for k in range(top):
        hit = routes[k] == expert
        named = named + jnp.where(hit, 1.0, 0.0)
        gate = gate + jnp.where(hit, gates[k], 0.0)
    row = lax.broadcasted_iota(jnp.int32, (rows, rows), 0)
    col = lax.broadcasted_iota(jnp.int32, (rows, rows), 1)
    rank = dot(named.astype(BF), jnp.where(row < col, 1.0, 0.0).astype(BF))
    row = lax.broadcasted_iota(jnp.int32, (experts, experts), 0)
    col = lax.broadcasted_iota(jnp.int32, (experts, experts), 1)
    limit = jnp.sum(jnp.where(row == col, capacity[...].astype(F32), 0.0), 1, keepdims=True)
    kept = (named > 0.5) & (rank < limit)
    depth = down.shape[0]
    out[0:depth, :] = down[...]
    out[depth : depth + experts, 0:rows] = jnp.where(kept, rank, -1.0).astype(BF)
    out[depth : depth + experts, rows : 2 * rows] = jnp.where(kept, gate, 0.0).astype(BF)


def unpack_body(depth, ids, *refs):
    halves, (down, meta) = refs[:-2], refs[-2:]
    chips = len(halves) // 2
    tall, wide = halves[0].shape
    experts = tall - depth
    row = lax.broadcasted_iota(jnp.int32, (experts, wide), 0)
    for i, half in enumerate(halves):
        side, k = divmod(i, chips)
        block = ids[side, k]
        down[pl.ds(pl.multiple_of(block * depth, 16), depth), :] = half[0:depth, :]
        table = half[depth:tall, :].astype(F32)
        own = jnp.sum(jnp.where(row == ids[2, 0], table, 0.0), 0, keepdims=True)
        meta[i : i + 1, :] = own
        meta[pl.ds(3 * chips + block, 1), :] = own
        if side == 0:
            meta[2 * chips + k : 2 * chips + k + 1, :] = jnp.sum(
                jnp.where(row == ids[2, 1], table, 0.0), 0, keepdims=True
            )


def arrive_body(packs, most, chips, meta, down, gain, *refs):
    count = sum(len(ks) for ks in packs)
    pieces, outs = refs[: 2 * count], refs[2 * count :]
    latents = outs[-1]
    rows = latents.shape[1]
    half = rows // 2
    at = 0
    for g, ks in enumerate(packs):
        for i, k in enumerate(ks):
            x = jnp.concatenate([pieces[2 * at][...], pieces[2 * at + 1][0:half, :]], 0)
            pick = jnp.concatenate(
                [slots_of(meta[j : j + 1, 0:rows], most) for j in (k, 2 * chips + k)], 0
            ).astype(BF)
            chosen = dot(pick, x).astype(BF)
            outs[2 * g][i] = chosen[:most]
            outs[2 * g + 1][i] = chosen[most:]
            raw = dot(x, down[...])
            scale = lax.rsqrt(jnp.mean(raw * raw, -1, keepdims=True) + 1e-06)
            latents[at] = (raw * scale * gain[...]).astype(BF)
            at += 1


def attend(rows, keys, masks, w_query):
    query = (dot(rows, w_query) * (rows.shape[1] ** -0.5)).astype(BF)
    scores = [dot_last(query, piece) for piece in keys]
    scores = [s if m is None else jnp.where(m, s, -1e30) for s, m in zip(scores, masks, strict=True)]
    peak = functools.reduce(jnp.maximum, [jnp.max(s, -1, keepdims=True) for s in scores])
    weights = [jnp.exp(s - peak) for s in scores]
    total = sum(jnp.sum(w, -1, keepdims=True) for w in weights)
    accum = sum(dot(w.astype(BF), piece) for w, piece in zip(weights, keys, strict=True))
    return (accum / total).astype(BF)


def reorder(attended, order):
    place = lax.broadcasted_iota(jnp.int32, (attended.shape[1], order.shape[1]), 0)
    return dot(attended, jnp.where(place == order, 1.0, 0.0).astype(BF)).astype(BF)


def attend_body(most, chips, counts, packs, ids, order, meta, w_query, *refs):
    latents, (att, lat) = refs[:-2], refs[-2:]
    rows = latents[0].shape[1]
    blocks = 2 * chips
    for side in (0, 1):
        for group, ks in enumerate(packs):
            for i, k in enumerate(ks):
                block = pl.multiple_of(ids[side, k] * rows, rows)
                lat[pl.ds(block, rows), :] = latents[side * len(packs) + group][i]
    token = lax.broadcasted_iota(jnp.int32, (most, rows), 1).astype(F32)
    for first in range(0, blocks, counts):
        latent, place = [], []
        for b in range(first, first + counts):
            pick = slots_of(meta[3 * chips + b : 3 * chips + b + 1, 0:rows], most)
            spot = jnp.sum(pick * token, -1, keepdims=True).astype(jnp.int32)
            place.append(spot + (b - first) * rows)
            latent.append(dot(pick.astype(BF), lat[b * rows : (b + 1) * rows, :]).astype(BF))
        place = jnp.concatenate(place, 0)
        key = lax.broadcasted_iota(jnp.int32, (1, counts * rows), 1)
        keys, masks = [lat[first * rows : (first + counts) * rows, :]], [key <= place]
        if first:
            keys.append(lat[0 : first * rows, :])
            masks.append(None)
        attended = attend(jnp.concatenate(latent, 0), keys, masks, w_query[...])
        attended = reorder(attended, order[...])
        for b in range(first, first + counts):
            at = pl.multiple_of(ids[3, b] * most, most)
            att[pl.ds(at, most), :] = attended[(b - first) * most : (b - first + 1) * most, :]


def expert_body(ks, most, chips, meta, att, out_a, out_b, gate_up, expert_down, *refs):
    chosen_refs, outs = refs[:-2], refs[-2:]
    rows = meta.shape[1] // 2
    hidden_width = expert_down.shape[0]
    shard = out_a.shape[0]
    attended, gate = [], []
    for side in (0, 1):
        for k in ks:
            at = side * chips + k
            pick = slots_of(meta[at : at + 1, 0:rows], most)
            gate.append(jnp.sum(pick * meta[at : at + 1, rows : 2 * rows], -1, keepdims=True))
            attended.append(att[at * most : (at + 1) * most, :])
    chosen = jnp.concatenate([ref[i] for ref in chosen_refs for i in range(ref.shape[0])], 0)
    attended = jnp.concatenate(attended, 0)
    hidden = dot(attended[:, :shard], out_a[...]) + dot(attended[:, shard:], out_b[...])
    hidden = (chosen.astype(F32) + hidden).astype(BF)
    both = dot(hidden, gate_up[...])
    inner = (jax.nn.silu(both[:, :hidden_width]) * both[:, hidden_width:]).astype(BF)
    result = (dot(inner, expert_down[...]) * jnp.concatenate(gate, 0)).astype(BF)
    for i in range(2 * len(ks)):
        outs[i // len(ks)][i % len(ks)] = result[i * most : (i + 1) * most]


def spread(k, at, most, chips, meta, mine, theirs, cols):
    rows = meta.shape[1] // 2
    one = slots_of(meta[k : k + 1, 0:rows], most).astype(BF)
    two = slots_of(meta[2 * chips + k : 2 * chips + k + 1, 0:rows], most).astype(BF)
    return dot_first(one, mine[at, :, cols]) + dot_first(two, theirs[at, :, cols])


def combine_body(k, at, most, chips, first, size, meta, mine, theirs, *refs):
    total = spread(k, at, most, chips, meta, mine, theirs, slice(first, first + size))
    if len(refs) > 1:
        total = total + refs[0][...].astype(F32)
    refs[-1][...] = total.astype(BF)


def own_body(at, most, chips, ids, order, meta, w_query, out_a, out_b, tokens, lat, mine, theirs, *outs):
    rows = tokens.shape[0]
    start = pl.multiple_of(ids[0, 0] * rows, rows)
    place = start + lax.broadcasted_iota(jnp.int32, (rows, 1), 0)
    key = lax.broadcasted_iota(jnp.int32, (1, lat.shape[0]), 1)
    attended = attend(lat[pl.ds(start, rows), :], [lat[...]], [key <= place], w_query[...])
    attended = reorder(attended, order[...])
    shard = out_a.shape[0]
    hidden = dot(attended[:, :shard], out_a[...]) + dot(attended[:, shard:], out_b[...])
    hidden = (tokens[...].astype(F32) + hidden).astype(BF).astype(F32)
    first = 0
    for out in outs:
        cols = slice(first, first + out.shape[1])
        total = spread(0, at, most, chips, meta, mine, theirs, cols)
        out[...] = (hidden[:, cols] + total).astype(BF)
        first += out.shape[1]


def final_body(*refs):
    ins, out = refs[:-1], refs[-1]
    first = 0
    for one, two in zip(ins[0::2], ins[1::2], strict=True):
        size = one.shape[1]
        out[:, first : first + size] = (one[...].astype(F32) + two[...].astype(F32)).astype(BF)
        first += size


def after(x, *others):
    return lax.optimization_barrier((x, *others))[0]


def on_device(
    tokens, routes, gates, capacity, w_down_kv, kv_gain, w_query, w_out, w_gate_up, w_expert_down
):
    pipes = lax.axis_size("pipe")
    owners = lax.axis_size("expert")
    chips = owners // 2
    me = lax.axis_index("expert")
    rows, width = tokens.shape[1:]
    top = routes.shape[2]
    latent = w_query.shape[1]
    depth = w_down_kv.shape[1]
    most = max(2, 4 * rows * top // (3 * owners))
    shape = jax.ShapeDtypeStruct

    ring, blocks = [], np.zeros((owners, chips), np.int32)
    for r in range(chips):
        even, odd = 2 * chip_at(r, chips), 2 * chip_at(r, chips) + 1
        ring.append((even, 2 * chip_at(r + 1, chips)))
        ring.append((odd, 2 * chip_at(r - 1, chips) + 1))
        for k in range(chips):
            blocks[even, k] = 2 * chip_at(r - k, chips)
            blocks[odd, k] = 2 * chip_at(r + k, chips) + 1
    step = lambda x: lax.ppermute(x, "expert", ring)
    sibling = lambda x: lax.ppermute(x, "expert", [(i, i ^ 1) for i in range(owners)])
    last = [
        (p * owners + a, ((p + 1) % pipes) * owners + b) for p in range(pipes) for a, b in ring
    ]
    onward = lambda x: lax.ppermute(x, "pipe", [(p, (p + 1) % pipes) for p in range(pipes)])

    table = np.zeros((owners, 4, owners), np.int32)
    for e in range(owners):
        both = np.concatenate([blocks[e], blocks[e ^ 1]])
        table[e, 0, :chips], table[e, 1, :chips] = blocks[e], blocks[e ^ 1]
        table[e, 2, :2] = (e, e ^ 1)
        table[e, 3, both] = np.arange(owners)
    ids = lax.dynamic_index_in_dim(jnp.asarray(table), me, 0, keepdims=False)
    shard = w_out.shape[1]
    order = (ids[:2, :chips].reshape(-1)[:, None] * shard + jnp.arange(shard)[None, :]).reshape(1, -1)

    half = rows // 2
    small = [
        call(pack_body, shape((depth + owners, latent), BF), [VMEM] * 4)(
            routes.transpose(2, 0, 1), gates.transpose(2, 0, 1), capacity, w_down_kv[0]
        )
    ]
    first = [tokens[0, :half]]
    second = [jnp.concatenate([tokens[0, half:], w_out[0]], 0)]
    arrived = []
    for _ in range(1, chips):
        for stream in (small, first, second):
            arrived.append(stream[-1])
            stream.append(step(after(stream[-1], *arrived[-3:-1])))
    down, meta = call(
        functools.partial(unpack_body, depth),
        (shape((owners * depth, latent), BF), shape((5 * chips, 2 * rows), F32)),
        [SMEM] + [VMEM] * owners,
        flops=LONG,
    )(ids, *small, *[sibling(x) for x in small])

    chunks = [(1, 2), (3, 0)] + [(k, k + 1) for k in range(4, chips, 2)]
    chosen = {}
    lat_a, lat_b, groups = [], [], []
    for whole in (range(chips - 1), (chips - 1,)):
        packs = [tuple(k for k in ks if k in whole) for ks in chunks]
        packs = [ks for ks in packs if ks]
        flat = [k for ks in packs for k in ks]
        *picked, lat = call(
            functools.partial(arrive_body, packs, most, chips),
            tuple(shape((len(ks), most, width), BF) for ks in packs for _ in (0, 1))
            + (shape((len(flat), rows, latent), BF),),
            [VMEM] * (3 + 2 * len(flat)),
            flops=LONG,
            limit=16,
        )(meta, down, kv_gain, *[x for k in flat for x in (first[k], second[k])])
        for i, ks in enumerate(packs):
            chosen[ks] = (picked[2 * i], sibling(picked[2 * i + 1]))
        lat_a.append(lat)
        lat_b.append(sibling(lat))
        groups.append(tuple(flat))
    out_a = jnp.concatenate([x[half:] for x in second], 0)
    out_b = sibling(out_a)
    att, lat = call(
        functools.partial(attend_body, most, chips, 4, groups),
        (shape((owners * most, latent), BF), shape((owners * rows, latent), BF)),
        [SMEM] + [VMEM] * (3 + 4),
        flops=LONG,
        limit=16,
    )(ids, order, meta, w_query[0], *lat_a, *lat_b)

    gate_up, expert_down = w_gate_up[0, 0], w_expert_down[0, 0]
    mine, theirs = {}, {}

    def expert(ks, *waits):
        packs = [part for part in chosen if set(part) <= set(ks)]
        packs = [part for k in ks for part in packs if part[0] == k]
        picked = [chosen[part][side] for side in (0, 1) for part in packs]
        result, away = call(
            functools.partial(expert_body, ks, most, chips),
            (shape((len(ks), most, width), BF),) * 2,
            [VMEM] * (6 + len(picked)),
            flops=LONG // 10,
            limit=16,
        )(after(meta, *waits), att, out_a, out_b, gate_up, expert_down, *picked)
        back = sibling(away)
        for i, k in enumerate(ks):
            mine[k], theirs[k] = (result, i), back

    pieces = [(0, width // 2), (width // 2, width - width // 2)]
    passing = [None] * len(pieces)
    expert(chunks[0])
    waiting = list(chunks[1:])
    for k in range(1, chips):
        totals = []
        for i, (start, size) in enumerate(pieces):
            more = [] if passing[i] is None else [passing[i]]
            if k == chips - 2 and more:
                more = [after(more[0], *kept)]
            total = call(
                functools.partial(combine_body, k, mine[k][1], most, chips, start, size),
                shape((rows, size), BF),
                [VMEM] * (3 + len(more)),
            )(meta, mine[k][0], theirs[k], *more)
            totals.append(total)
            if k < chips - 1:
                passing[i] = step(total)
            else:
                passing[i] = lax.ppermute(total, ("pipe", "expert"), last)
        if waiting and k + 2 >= waiting[0][0]:
            expert(waiting.pop(0), totals[0])
        if k == 2:
            kept = call(
                functools.partial(own_body, mine[0][1], most, chips),
                tuple(shape((rows, size), BF) for _, size in pieces),
                [SMEM] + [VMEM] * 9,
            )(
                ids,
                order,
                meta,
                w_query[0],
                out_a,
                out_b,
                after(tokens[0], *totals),
                lat,
                mine[0][0],
                theirs[0],
            )
            passing = [after(x, *kept) for x in passing]
            kept = [onward(x) for x in kept]
    output = call(final_body, shape((rows, width), BF), [VMEM] * (2 * len(pieces)))(
        *[x for pair in zip(kept, passing, strict=True) for x in pair]
    )
    return output[None]


def solution(mesh):
    return jax.shard_map(
        on_device,
        mesh=mesh,
        in_specs=(
            P("pipe", "expert", None),
            P("pipe", "expert", None),
            P("pipe", "expert", None),
            P("pipe", None),
            P("pipe", "expert", None),
            P("pipe", None),
            P("pipe", None, None),
            P("pipe", "expert", None),
            P("pipe", "expert", None, None),
            P("pipe", "expert", None, None),
        ),
        out_specs=P("pipe", "expert", None),
        check_vma=False,
    )
```

```python
import functools

import jax
import jax.numpy as jnp
import numpy as np
from jax import lax
from jax.experimental import pallas as pl
from jax.experimental.pallas import tpu as pltpu
from jax.sharding import PartitionSpec as P

BF = jnp.bfloat16
F32 = jnp.float32
VMEM = pl.BlockSpec(memory_space=pltpu.VMEM)
SMEM = pl.BlockSpec(memory_space=pltpu.SMEM)
MIB = 1024 * 1024
LONG = 10**11
SHORT = 3 * 10**9


def chip_at(place, chips):
    place %= chips
    half = chips // 2
    return 2 * place if place < half else 2 * (chips - 1 - place) + 1


def call(body, outs, ins, limit=12, flops=0, moved=None):
    return pl.pallas_call(
        body,
        out_shape=outs,
        in_specs=ins,
        out_specs=jax.tree.map(lambda _: VMEM, outs),
        compiler_params=pltpu.CompilerParams(vmem_limit_bytes=limit * MIB),
        cost_estimate=pl.CostEstimate(
            flops=flops, transcendentals=0, bytes_accessed=flops // 100 if moved is None else moved
        ),
    )


def dot(a, b):
    return jnp.dot(a, b, preferred_element_type=F32)


def dot_first(a, b):
    return lax.dot_general(a, b, (((0,), (0,)), ((), ())), preferred_element_type=F32)


def dot_last(a, b):
    return lax.dot_general(a, b, (((1,), (1,)), ((), ())), preferred_element_type=F32)


def slots_of(row, most):
    ids = lax.broadcasted_iota(jnp.int32, (most, row.shape[1]), 0).astype(F32)
    return jnp.where(ids == row, 1.0, 0.0)


def pack_body(tokens, routes, gates, capacity, down, out, first, second):
    top, _, rows = routes.shape
    experts = capacity.shape[1]
    latent = down.shape[1]
    half = rows // 2
    for j in range(tokens.shape[1] // latent):
        first[j * half : (j + 1) * half, :] = tokens[0:half, j * latent : (j + 1) * latent]
    second[0:half, :] = tokens[half:rows, :]
    second[half : half + out.shape[0], :] = out[...]
    expert = lax.broadcasted_iota(jnp.int32, (experts, rows), 0)
    named = jnp.zeros((experts, rows), F32)
    gate = jnp.zeros((experts, rows), F32)
    for k in range(top):
        hit = routes[k] == expert
        named = named + jnp.where(hit, 1.0, 0.0)
        gate = gate + jnp.where(hit, gates[k], 0.0)
    row = lax.broadcasted_iota(jnp.int32, (rows, rows), 0)
    col = lax.broadcasted_iota(jnp.int32, (rows, rows), 1)
    rank = dot(named.astype(BF), jnp.where(row < col, 1.0, 0.0).astype(BF))
    row = lax.broadcasted_iota(jnp.int32, (experts, experts), 0)
    col = lax.broadcasted_iota(jnp.int32, (experts, experts), 1)
    limit = jnp.sum(jnp.where(row == col, capacity[...].astype(F32), 0.0), 1, keepdims=True)
    kept = (named > 0.5) & (rank < limit)
    start = tokens.shape[1] // latent * half
    first[start : start + down.shape[0], :] = down[...]
    start += down.shape[0]
    first[start : start + experts, 0:rows] = jnp.where(kept, rank, -1.0).astype(BF)
    first[start : start + experts, rows : 2 * rows] = jnp.where(kept, gate, 0.0).astype(BF)


def tail_body(piece, out):
    out[...] = piece[piece.shape[0] - out.shape[0] :, :]


def stack_body(*refs):
    ins, out = refs[:-1], refs[-1]
    for i, piece in enumerate(ins):
        out[i] = piece[...]


def unpack_body(depth, ids, *refs):
    arrays, (down, meta) = refs[:-2], refs[-2:]
    halves = [ref.at[i] for ref in arrays for i in range(ref.shape[0])]
    chips = len(halves) // 2
    tall, wide = halves[0].shape
    experts = tall - depth
    row = lax.broadcasted_iota(jnp.int32, (experts, wide), 0)
    for i, half in enumerate(halves):
        side, k = divmod(i, chips)
        block = ids[side, k]
        down[pl.ds(pl.multiple_of(block * depth, 16), depth), :] = half[0:depth, :]
        table = half[depth:tall, :].astype(F32)
        own = jnp.sum(jnp.where(row == ids[2, 0], table, 0.0), 0, keepdims=True)
        meta[i : i + 1, :] = own
        meta[pl.ds(3 * chips + block, 1), :] = own
        if side == 0:
            meta[2 * chips + k : 2 * chips + k + 1, :] = jnp.sum(
                jnp.where(row == ids[2, 1], table, 0.0), 0, keepdims=True
            )


def arrive_body(packs, most, chips, meta, down, gain, *refs):
    count = sum(len(ks) for ks in packs)
    pieces, outs = refs[: 2 * count], refs[2 * count :]
    latents = outs[-1]
    rows, latent = latents.shape[1:]
    half = rows // 2
    at = 0
    for g, ks in enumerate(packs):
        for i, k in enumerate(ks):
            one, two = pieces[2 * at], pieces[2 * at + 1]
            blocks = range(two.shape[1] // latent)
            one = jnp.concatenate([one[j * half : (j + 1) * half, :] for j in blocks], 1)
            x = jnp.concatenate([one, two[0:half, :]], 0)
            pick = jnp.concatenate(
                [slots_of(meta[j : j + 1, 0:rows], most) for j in (k, 2 * chips + k)], 0
            ).astype(BF)
            chosen = dot(pick, x).astype(BF)
            outs[2 * g][i] = chosen[:most]
            outs[2 * g + 1][i] = chosen[most:]
            raw = dot(x, down[...])
            scale = lax.rsqrt(jnp.mean(raw * raw, -1, keepdims=True) + 1e-06)
            latents[at] = (raw * scale * gain[...]).astype(BF)
            at += 1


def attend(rows, keys, masks, w_query):
    query = (dot(rows, w_query) * (rows.shape[1] ** -0.5)).astype(BF)
    scores = [dot_last(query, piece) for piece in keys]
    scores = [s if m is None else jnp.where(m, s, -1e30) for s, m in zip(scores, masks, strict=True)]
    peak = functools.reduce(jnp.maximum, [jnp.max(s, -1, keepdims=True) for s in scores])
    weights = [jnp.exp(s - peak) for s in scores]
    total = sum(jnp.sum(w, -1, keepdims=True) for w in weights)
    accum = sum(dot(w.astype(BF), piece) for w, piece in zip(weights, keys, strict=True))
    return (accum / total).astype(BF)


def reorder(attended, order):
    place = lax.broadcasted_iota(jnp.int32, (attended.shape[1], order.shape[1]), 0)
    return dot(attended, jnp.where(place == order, 1.0, 0.0).astype(BF)).astype(BF)


def attend_body(most, chips, counts, packs, ids, order, meta, w_query, *refs):
    latents, (att, lat) = refs[:-2], refs[-2:]
    rows = latents[0].shape[1]
    blocks = 2 * chips
    for side in (0, 1):
        for group, ks in enumerate(packs):
            for i, k in enumerate(ks):
                block = pl.multiple_of(ids[side, k] * rows, rows)
                lat[pl.ds(block, rows), :] = latents[side * len(packs) + group][i]
    token = lax.broadcasted_iota(jnp.int32, (most, rows), 1).astype(F32)
    for first in range(0, blocks, counts):
        latent, place = [], []
        for b in range(first, first + counts):
            pick = slots_of(meta[3 * chips + b : 3 * chips + b + 1, 0:rows], most)
            spot = jnp.sum(pick * token, -1, keepdims=True).astype(jnp.int32)
            place.append(spot + (b - first) * rows)
            latent.append(dot(pick.astype(BF), lat[b * rows : (b + 1) * rows, :]).astype(BF))
        place = jnp.concatenate(place, 0)
        key = lax.broadcasted_iota(jnp.int32, (1, counts * rows), 1)
        keys, masks = [lat[first * rows : (first + counts) * rows, :]], [key <= place]
        if first:
            keys.append(lat[0 : first * rows, :])
            masks.append(None)
        attended = attend(jnp.concatenate(latent, 0), keys, masks, w_query[...])
        attended = reorder(attended, order[...])
        for b in range(first, first + counts):
            at = pl.multiple_of(ids[3, b] * most, most)
            att[pl.ds(at, most), :] = attended[(b - first) * most : (b - first + 1) * most, :]


def expert_body(ks, most, chips, meta, att, out_a, out_b, gate_up, expert_down, *refs):
    chosen_refs, outs = refs[:-2], refs[-2:]
    rows = meta.shape[1] // 2
    hidden_width = expert_down.shape[0]
    shard = out_a.shape[0]
    attended, gate = [], []
    for side in (0, 1):
        for k in ks:
            at = side * chips + k
            pick = slots_of(meta[at : at + 1, 0:rows], most)
            gate.append(jnp.sum(pick * meta[at : at + 1, rows : 2 * rows], -1, keepdims=True))
            attended.append(att[at * most : (at + 1) * most, :])
    chosen = jnp.concatenate([ref[i] for ref in chosen_refs for i in range(ref.shape[0])], 0)
    attended = jnp.concatenate(attended, 0)
    hidden = dot(attended[:, :shard], out_a[...]) + dot(attended[:, shard:], out_b[...])
    hidden = (chosen.astype(F32) + hidden).astype(BF)
    both = dot(hidden, gate_up[...])
    inner = (jax.nn.silu(both[:, :hidden_width]) * both[:, hidden_width:]).astype(BF)
    result = (dot(inner, expert_down[...]) * jnp.concatenate(gate, 0)).astype(BF)
    for i in range(2 * len(ks)):
        outs[i // len(ks)][i % len(ks)] = result[i * most : (i + 1) * most]


def spread(k, at, most, chips, meta, mine, theirs, cols):
    rows = meta.shape[1] // 2
    one = slots_of(meta[k : k + 1, 0:rows], most).astype(BF)
    two = slots_of(meta[2 * chips + k : 2 * chips + k + 1, 0:rows], most).astype(BF)
    return dot_first(one, mine[at, :, cols]) + dot_first(two, theirs[at, :, cols])


def combine_body(k, at, most, chips, first, size, meta, mine, theirs, *refs):
    total = spread(k, at, most, chips, meta, mine, theirs, slice(first, first + size))
    if len(refs) > 1:
        total = total + refs[0][...].astype(F32)
    refs[-1][...] = total.astype(BF)


def own_body(at, most, chips, ids, order, meta, w_query, out_a, out_b, tokens, lat, mine, theirs, *outs):
    rows = tokens.shape[0]
    start = pl.multiple_of(ids[0, 0] * rows, rows)
    place = start + lax.broadcasted_iota(jnp.int32, (rows, 1), 0)
    key = lax.broadcasted_iota(jnp.int32, (1, lat.shape[0]), 1)
    attended = attend(lat[pl.ds(start, rows), :], [lat[...]], [key <= place], w_query[...])
    attended = reorder(attended, order[...])
    shard = out_a.shape[0]
    hidden = dot(attended[:, :shard], out_a[...]) + dot(attended[:, shard:], out_b[...])
    hidden = (tokens[...].astype(F32) + hidden).astype(BF).astype(F32)
    first = 0
    for out in outs:
        cols = slice(first, first + out.shape[1])
        total = spread(0, at, most, chips, meta, mine, theirs, cols)
        out[...] = (hidden[:, cols] + total).astype(BF)
        first += out.shape[1]


def final_body(*refs):
    ins, out = refs[:-1], refs[-1]
    first = 0
    for one, two in zip(ins[0::2], ins[1::2], strict=True):
        size = one.shape[1]
        out[:, first : first + size] = (one[...].astype(F32) + two[...].astype(F32)).astype(BF)
        first += size


def after(x, *others):
    return lax.optimization_barrier((x, *others))[0]


def on_device(
    tokens, routes, gates, capacity, w_down_kv, kv_gain, w_query, w_out, w_gate_up, w_expert_down
):
    pipes = lax.axis_size("pipe")
    owners = lax.axis_size("expert")
    chips = owners // 2
    me = lax.axis_index("expert")
    rows, width = tokens.shape[1:]
    top = routes.shape[2]
    latent = w_query.shape[1]
    depth = w_down_kv.shape[1]
    most = max(2, 4 * rows * top // (3 * owners))
    shape = jax.ShapeDtypeStruct

    ring, blocks = [], np.zeros((owners, chips), np.int32)
    for r in range(chips):
        even, odd = 2 * chip_at(r, chips), 2 * chip_at(r, chips) + 1
        ring.append((even, 2 * chip_at(r + 1, chips)))
        ring.append((odd, 2 * chip_at(r - 1, chips) + 1))
        for k in range(chips):
            blocks[even, k] = 2 * chip_at(r - k, chips)
            blocks[odd, k] = 2 * chip_at(r + k, chips) + 1
    step = lambda x: lax.ppermute(x, "expert", ring)
    sibling = lambda x: lax.ppermute(x, "expert", [(i, i ^ 1) for i in range(owners)])
    last = [
        (p * owners + a, ((p + 1) % pipes) * owners + b) for p in range(pipes) for a, b in ring
    ]
    onward = lambda x: lax.ppermute(x, "pipe", [(p, (p + 1) % pipes) for p in range(pipes)])

    table = np.zeros((owners, 4, owners), np.int32)
    for e in range(owners):
        both = np.concatenate([blocks[e], blocks[e ^ 1]])
        table[e, 0, :chips], table[e, 1, :chips] = blocks[e], blocks[e ^ 1]
        table[e, 2, :2] = (e, e ^ 1)
        table[e, 3, both] = np.arange(owners)
    ids = lax.dynamic_index_in_dim(jnp.asarray(table), me, 0, keepdims=False)
    shard = w_out.shape[1]
    order = (ids[:2, :chips].reshape(-1)[:, None] * shard + jnp.arange(shard)[None, :]).reshape(1, -1)

    half = rows // 2
    tall = depth + owners
    one, two = call(
        pack_body,
        (
            shape((width // latent * half + tall, latent), BF),
            shape((half + shard, width), BF),
        ),
        [VMEM] * 6,
    )(
        tokens[0],
        routes.transpose(2, 0, 1),
        gates.transpose(2, 0, 1),
        capacity,
        w_down_kv[0],
        w_out[0],
    )
    def tail(x, rows, *others):
        return call(tail_body, shape((rows, x.shape[1]), BF), [VMEM], flops=SHORT, moved=0)(
            after(x, *others)
        )

    first, second = [one], [two]
    small = [tail(one, tall)]
    outs = [tail(two, shard, small[0])]
    for k in range(1, chips):
        first.append(step(after(first[-1], *outs[k - 2 : k - 1])))
        second.append(step(after(second[-1], small[k - 1])))
        small.append(tail(first[k], tall, outs[k - 1]))
        outs.append(tail(second[k], shard, small[k]))
    stack = lambda xs: call(stack_body, shape((len(xs), *xs[0].shape), BF), [VMEM] * len(xs))(*xs)
    small = [stack(small[:-1]), stack(small[-1:])]
    down, meta = call(
        functools.partial(unpack_body, depth),
        (shape((owners * depth, latent), BF), shape((5 * chips, 2 * rows), F32)),
        [SMEM] + [VMEM] * 4,
        flops=LONG,
    )(ids, *small, *[sibling(x) for x in small])

    chunks = [(1, 2), (3, 0)] + [(k, k + 1) for k in range(4, chips, 2)]
    chosen = {}
    lat_a, lat_b, groups = [], [], []
    for whole in (range(chips - 1), (chips - 1,)):
        packs = [tuple(k for k in ks if k in whole) for ks in chunks]
        packs = [ks for ks in packs if ks]
        flat = [k for ks in packs for k in ks]
        *picked, lat = call(
            functools.partial(arrive_body, packs, most, chips),
            tuple(shape((len(ks), most, width), BF) for ks in packs for _ in (0, 1))
            + (shape((len(flat), rows, latent), BF),),
            [VMEM] * (3 + 2 * len(flat)),
            flops=LONG,
            limit=16,
        )(meta, down, kv_gain, *[x for k in flat for x in (first[k], second[k])])
        for i, ks in enumerate(packs):
            chosen[ks] = (picked[2 * i], sibling(picked[2 * i + 1]))
        lat_a.append(lat)
        lat_b.append(sibling(lat))
        groups.append(tuple(flat))
    out_a = stack(outs).reshape(-1, width)
    out_b = sibling(out_a)
    att, lat = call(
        functools.partial(attend_body, most, chips, 4, groups),
        (shape((owners * most, latent), BF), shape((owners * rows, latent), BF)),
        [SMEM] + [VMEM] * (3 + 4),
        flops=LONG,
        limit=16,
    )(ids, order, meta, w_query[0], *lat_a, *lat_b)

    gate_up, expert_down = w_gate_up[0, 0], w_expert_down[0, 0]
    mine, theirs = {}, {}

    def expert(ks, *waits):
        packs = [part for part in chosen if set(part) <= set(ks)]
        packs = [part for k in ks for part in packs if part[0] == k]
        picked = [chosen[part][side] for side in (0, 1) for part in packs]
        result, away = call(
            functools.partial(expert_body, ks, most, chips),
            (shape((len(ks), most, width), BF),) * 2,
            [VMEM] * (6 + len(picked)),
            flops=LONG // 10,
            limit=16,
        )(after(meta, *waits), att, out_a, out_b, gate_up, expert_down, *picked)
        back = sibling(away)
        for i, k in enumerate(ks):
            mine[k], theirs[k] = (result, i), back

    pieces = [(0, width // 2), (width // 2, width - width // 2)]
    passing = [None] * len(pieces)
    expert(chunks[0])
    waiting = list(chunks[1:])
    def combine(k, i, *more):
        start, size = pieces[i]
        return call(
            functools.partial(combine_body, k, mine[k][1], most, chips, start, size),
            shape((rows, size), BF),
            [VMEM] * (3 + len(more)),
        )(meta, mine[k][0], theirs[k], *more)

    cross = lambda x: lax.ppermute(x, ("pipe", "expert"), last)
    for k in range(1, chips):
        totals = []
        for i in range(len(pieces)):
            more = [] if k == 1 else [passing[i]]
            if i == 0 and chips - 3 <= k < chips - 1:
                more = [after(more[0], kept[k - (chips - 3)])]
            totals.append(combine(k, i, *more))
            passing[i] = (cross if k == chips - 1 else step)(totals[i])
        if waiting and k + 3 >= waiting[0][0]:
            expert(waiting.pop(0), totals[0])
        if k == 2:
            kept = call(
                functools.partial(own_body, mine[0][1], most, chips),
                tuple(shape((rows, size), BF) for _, size in pieces),
                [SMEM] + [VMEM] * 9,
            )(
                ids,
                order,
                meta,
                w_query[0],
                out_a,
                out_b,
                after(tokens[0], *totals),
                lat,
                mine[0][0],
                theirs[0],
            )
            passing = [after(x, *kept) for x in passing]
            kept = [onward(x) for x in kept]
    output = call(final_body, shape((rows, width), BF), [VMEM] * (2 * len(pieces)))(
        *[x for pair in zip(kept, passing, strict=True) for x in pair]
    )
    return output[None]


def solution(mesh):
    return jax.shard_map(
        on_device,
        mesh=mesh,
        in_specs=(
            P("pipe", "expert", None),
            P("pipe", "expert", None),
            P("pipe", "expert", None),
            P("pipe", None),
            P("pipe", "expert", None),
            P("pipe", None),
            P("pipe", None, None),
            P("pipe", "expert", None),
            P("pipe", "expert", None, None),
            P("pipe", "expert", None, None),
        ),
        out_specs=P("pipe", "expert", None),
        check_vma=False,
    )
```

```python
import functools

import jax
import jax.numpy as jnp
import numpy as np
from jax import lax
from jax.experimental import pallas as pl
from jax.experimental.pallas import tpu as pltpu
from jax.sharding import PartitionSpec as P

BF = jnp.bfloat16
F32 = jnp.float32
VMEM = pl.BlockSpec(memory_space=pltpu.VMEM)
SMEM = pl.BlockSpec(memory_space=pltpu.SMEM)
MIB = 1024 * 1024
LONG = 10**10
SHORT = 3 * 10**9


def chip_at(place, chips):
    place %= chips
    half = chips // 2
    return 2 * place if place < half else 2 * (chips - 1 - place) + 1


def call(body, outs, ins, limit=8, flops=0, moved=None):
    return pl.pallas_call(
        body,
        out_shape=outs,
        in_specs=ins,
        out_specs=jax.tree.map(lambda _: VMEM, outs),
        compiler_params=pltpu.CompilerParams(vmem_limit_bytes=limit * MIB),
        cost_estimate=pl.CostEstimate(
            flops=flops, transcendentals=0, bytes_accessed=flops // 100 if moved is None else moved
        ),
    )


def dot(a, b):
    return jnp.dot(a, b, preferred_element_type=F32)


def dot_first(a, b):
    return lax.dot_general(a, b, (((0,), (0,)), ((), ())), preferred_element_type=F32)


def dot_last(a, b):
    return lax.dot_general(a, b, (((1,), (1,)), ((), ())), preferred_element_type=F32)


def slots_of(row, most):
    ids = lax.broadcasted_iota(jnp.int32, (most, row.shape[1]), 0).astype(F32)
    return jnp.where(ids == row, 1.0, 0.0)


def blocks_of(x, out, first, latent):
    size = x.shape[0]
    for j in range(x.shape[1] // latent):
        out[first + j * size : first + (j + 1) * size, :] = x[:, j * latent : (j + 1) * latent]


def joined(piece, first, size, count):
    return jnp.concatenate(
        [piece[first + j * size : first + (j + 1) * size, :] for j in range(count)], 1
    )


def pack_weights_body(down, out, weights):
    weights[0 : down.shape[0], :] = down[...]
    blocks_of(out[...], weights, down.shape[0], down.shape[1])


def pack_first_body(tokens, weights, first):
    latent = weights.shape[1]
    blocks_of(tokens[0 : tokens.shape[0] // 2, :], first, 0, latent)
    first[first.shape[0] - weights.shape[0] :, :] = weights[...]


def head_body(piece, out):
    out[...] = piece[0 : out.shape[0], :]


def last_body(piece, out):
    out[...] = piece[piece.shape[0] - out.shape[0] :, :]


def pack_second_body(tokens, routes, gates, capacity, second):
    top, _, rows = routes.shape
    experts = capacity.shape[1]
    half = rows // 2
    latent = second.shape[1]
    blocks_of(tokens[half:rows, :], second, 0, latent)
    expert = lax.broadcasted_iota(jnp.int32, (experts, rows), 0)
    named = jnp.zeros((experts, rows), F32)
    gate = jnp.zeros((experts, rows), F32)
    for k in range(top):
        hit = routes[k] == expert
        named = named + jnp.where(hit, 1.0, 0.0)
        gate = gate + jnp.where(hit, gates[k], 0.0)
    row = lax.broadcasted_iota(jnp.int32, (rows, rows), 0)
    col = lax.broadcasted_iota(jnp.int32, (rows, rows), 1)
    rank = dot(named.astype(BF), jnp.where(row < col, 1.0, 0.0).astype(BF))
    row = lax.broadcasted_iota(jnp.int32, (experts, experts), 0)
    col = lax.broadcasted_iota(jnp.int32, (experts, experts), 1)
    limit = jnp.sum(jnp.where(row == col, capacity[...].astype(F32), 0.0), 1, keepdims=True)
    kept = (named > 0.5) & (rank < limit)
    start = half * (tokens.shape[1] // latent)
    second[start : start + experts, 0:rows] = jnp.where(kept, rank, -1.0).astype(BF)
    second[start : start + experts, rows : 2 * rows] = jnp.where(kept, gate, 0.0).astype(BF)


def tail_body(piece, down, out):
    count = out.shape[1] // piece.shape[1]
    end = piece.shape[0] - out.shape[0] * count
    down[...] = piece[end - down.shape[0] : end, :]
    out[...] = joined(piece, end, out.shape[0], count)


def stack_body(*refs):
    ins, out = refs[:-1], refs[-1]
    for i, piece in enumerate(ins):
        out[i] = piece[...]


def unpack_body(ids, *refs):
    arrays, down = refs[:-1], refs[-1]
    halves = [ref.at[i] for ref in arrays for i in range(ref.shape[0])]
    chips = len(halves) // 2
    depth = halves[0].shape[0]
    for i, half in enumerate(halves):
        side, k = divmod(i, chips)
        down[pl.ds(pl.multiple_of(ids[side, k] * depth, 16), depth), :] = half[...]


def table_body(ids, *refs):
    arrays, meta = refs[:-1], refs[-1]
    halves = [ref.at[i] for ref in arrays for i in range(ref.shape[0])]
    chips = len(halves) // 2
    row = lax.broadcasted_iota(jnp.int32, halves[0].shape, 0)
    for i, half in enumerate(halves):
        side, k = divmod(i, chips)
        table = half[...].astype(F32)
        own = jnp.sum(jnp.where(row == ids[2, 0], table, 0.0), 0, keepdims=True)
        meta[i : i + 1, :] = own
        meta[pl.ds(3 * chips + ids[side, k], 1), :] = own
        if side == 0:
            meta[2 * chips + k : 2 * chips + k + 1, :] = jnp.sum(
                jnp.where(row == ids[2, 1], table, 0.0), 0, keepdims=True
            )


def whole(one, two, rows, count):
    half = rows // 2
    return jnp.concatenate([joined(one, 0, half, count), joined(two, 0, half, count)], 0)


def choose_body(most, ids, small, one, two, *refs):
    lines, (own, other) = refs[:-2], refs[-2:]
    latent = two.shape[1]
    rows = latent // 2
    table = small[...].astype(F32)
    row = lax.broadcasted_iota(jnp.int32, (small.shape[0], rows), 0)
    picks = []
    for which in (0, 1):
        mine = jnp.where(row == ids[2, which], table[:, 0:rows], 0.0)
        picks.append(slots_of(jnp.sum(mine, 0, keepdims=True), most))
    tokens = whole(one, two, rows, own.shape[1] // latent)
    chosen = dot(jnp.concatenate(picks, 0).astype(BF), tokens)
    own[...] = chosen[:most].astype(BF)
    other[0:most, :] = chosen[most:].astype(BF)
    start = most
    for line in lines:
        other[start : start + line.shape[0], :] = line[...]
        start += line.shape[0]


def gate_up_body(count, gate_up, *refs):
    result = dot(jnp.concatenate([ref[...] for ref in refs[:count]], 0), gate_up[...]).astype(BF)
    start = 0
    for out in refs[count:]:
        out[...] = result[start : start + out.shape[0]]
        start += out.shape[0]


def latent_body(down, gain, *refs):
    pieces, latents = refs[:-1], refs[-1]
    rows, latent = latents.shape[1:]
    for i in range(latents.shape[0]):
        x = whole(pieces[2 * i], pieces[2 * i + 1], rows, down.shape[0] // latent)
        raw = dot(x, down[...])
        scale = lax.rsqrt(jnp.mean(raw * raw, -1, keepdims=True) + 1e-06)
        latents[i] = (raw * scale * gain[...]).astype(BF)


def attend(rows, keys, masks, w_query):
    query = (dot(rows, w_query) * (rows.shape[1] ** -0.5)).astype(BF)
    scores = [dot_last(query, piece) for piece in keys]
    scores = [s if m is None else jnp.where(m, s, -1e30) for s, m in zip(scores, masks, strict=True)]
    peak = functools.reduce(jnp.maximum, [jnp.max(s, -1, keepdims=True) for s in scores])
    weights = [jnp.exp(s - peak) for s in scores]
    total = sum(jnp.sum(w, -1, keepdims=True) for w in weights)
    accum = sum(dot(w.astype(BF), piece) for w, piece in zip(weights, keys, strict=True))
    return (accum / total).astype(BF)


def reorder(attended, order):
    place = lax.broadcasted_iota(jnp.int32, (attended.shape[1], order.shape[1]), 0)
    return dot(attended, jnp.where(place == order[4:5, :], 1.0, 0.0).astype(BF)).astype(BF)


def attend_body(most, chips, counts, packs, ids, order, meta, w_query, *refs):
    latents, (att, lat) = refs[:-2], refs[-2:]
    rows = latents[0].shape[1]
    blocks = 2 * chips
    for side in (0, 1):
        for group, ks in enumerate(packs):
            for i, k in enumerate(ks):
                block = pl.multiple_of(ids[side, k] * rows, rows)
                lat[pl.ds(block, rows), :] = latents[side * len(packs) + group][i]
    token = lax.broadcasted_iota(jnp.int32, (most, rows), 1).astype(F32)
    for first in range(0, blocks, counts):
        latent, place = [], []
        for b in range(first, first + counts):
            pick = slots_of(meta[3 * chips + b : 3 * chips + b + 1, 0:rows], most)
            spot = jnp.sum(pick * token, -1, keepdims=True).astype(jnp.int32)
            place.append(spot + (b - first) * rows)
            latent.append(dot(pick.astype(BF), lat[b * rows : (b + 1) * rows, :]).astype(BF))
        place = jnp.concatenate(place, 0)
        key = lax.broadcasted_iota(jnp.int32, (1, counts * rows), 1)
        keys, masks = [lat[first * rows : (first + counts) * rows, :]], [key <= place]
        if first:
            keys.append(lat[0 : first * rows, :])
            masks.append(None)
        attended = attend(jnp.concatenate(latent, 0), keys, masks, w_query[...])
        attended = reorder(attended, order[...])
        for b in range(first, first + counts):
            at = pl.multiple_of(ids[3, b] * most, most)
            att[pl.ds(at, most), :] = attended[(b - first) * most : (b - first + 1) * most, :]


def expert_body(ks, most, chips, meta, att, wide_a, wide_b, expert_down, *refs):
    chosen, outs = refs[:-2], refs[-2:]
    rows = meta.shape[1] // 2
    hidden_width = expert_down.shape[0]
    shard = wide_a.shape[0]
    attended, gate = [], []
    for side in (0, 1):
        for k in ks:
            at = side * chips + k
            pick = slots_of(meta[at : at + 1, 0:rows], most)
            gate.append(jnp.sum(pick * meta[at : at + 1, rows : 2 * rows], -1, keepdims=True))
            attended.append(att[at * most : (at + 1) * most, :])
    attended = jnp.concatenate(attended, 0)
    both = dot(attended[:, :shard], wide_a[...]) + dot(attended[:, shard:], wide_b[...])
    both = both + jnp.concatenate([ref[...] for ref in chosen], 0).astype(F32)
    inner = (jax.nn.silu(both[:, :hidden_width]) * both[:, hidden_width:]).astype(BF)
    result = (dot(inner, expert_down[...]) * jnp.concatenate(gate, 0)).astype(BF)
    for i in range(2 * len(ks)):
        outs[i // len(ks)][i % len(ks)] = result[i * most : (i + 1) * most]


def spread(k, at, most, chips, meta, mine, theirs, cols):
    rows = meta.shape[1] // 2
    one = slots_of(meta[k : k + 1, 0:rows], most).astype(BF)
    two = slots_of(meta[2 * chips + k : 2 * chips + k + 1, 0:rows], most).astype(BF)
    return dot_first(one, mine[at, :, cols]) + dot_first(two, theirs[at, :, cols])


def combine_body(k, at, most, chips, first, size, meta, mine, theirs, *refs):
    total = spread(k, at, most, chips, meta, mine, theirs, slice(first, first + size))
    if len(refs) > 1:
        total = total + refs[0][...].astype(F32)
    refs[-1][...] = total.astype(BF)


def own_body(at, most, chips, ids, order, meta, w_query, out_a, out_b, tokens, lat, mine, theirs, *outs):
    rows = tokens.shape[0]
    start = pl.multiple_of(ids[0, 0] * rows, rows)
    place = start + lax.broadcasted_iota(jnp.int32, (rows, 1), 0)
    key = lax.broadcasted_iota(jnp.int32, (1, lat.shape[0]), 1)
    attended = attend(lat[pl.ds(start, rows), :], [lat[...]], [key <= place], w_query[...])
    attended = reorder(attended, order[...])
    shard = out_a.shape[0]
    hidden = dot(attended[:, :shard], out_a[...]) + dot(attended[:, shard:], out_b[...])
    hidden = (tokens[...].astype(F32) + hidden).astype(BF).astype(F32)
    first = 0
    for out in outs:
        cols = slice(first, first + out.shape[1])
        total = spread(0, at, most, chips, meta, mine, theirs, cols)
        out[...] = (hidden[:, cols] + total).astype(BF)
        first += out.shape[1]


def add_body(one, two, out):
    out[...] = (one[...].astype(F32) + two[...].astype(F32)).astype(BF)


def final_body(first, one, two, out):
    size = first.shape[1]
    out[:, :size] = first[...]
    out[:, size:] = (one[...].astype(F32) + two[...].astype(F32)).astype(BF)


def after(x, *others):
    return lax.optimization_barrier((x, *others))[0]


def on_device(
    tokens, routes, gates, capacity, w_down_kv, kv_gain, w_query, w_out, w_gate_up, w_expert_down
):
    pipes = lax.axis_size("pipe")
    owners = lax.axis_size("expert")
    chips = owners // 2
    me = lax.axis_index("expert")
    rows, width = tokens.shape[1:]
    top = routes.shape[2]
    latent = w_query.shape[1]
    depth = w_down_kv.shape[1]
    most = max(2, 4 * rows * top // (3 * owners))
    shape = jax.ShapeDtypeStruct

    ring, blocks = [], np.zeros((owners, chips), np.int32)
    for r in range(chips):
        even, odd = 2 * chip_at(r, chips), 2 * chip_at(r, chips) + 1
        ring.append((even, 2 * chip_at(r + 1, chips)))
        ring.append((odd, 2 * chip_at(r - 1, chips) + 1))
        for k in range(chips):
            blocks[even, k] = 2 * chip_at(r - k, chips)
            blocks[odd, k] = 2 * chip_at(r + k, chips) + 1
    step = lambda x: lax.ppermute(x, "expert", ring)
    sibling = lambda x: lax.ppermute(x, "expert", [(i, i ^ 1) for i in range(owners)])
    last = [
        (p * owners + a, ((p + 1) % pipes) * owners + b) for p in range(pipes) for a, b in ring
    ]
    onward = lambda x: lax.ppermute(x, "pipe", [(p, (p + 1) % pipes) for p in range(pipes)])

    table = np.zeros((owners, 4, owners), np.int32)
    for e in range(owners):
        both = np.concatenate([blocks[e], blocks[e ^ 1]])
        table[e, 0, :chips], table[e, 1, :chips] = blocks[e], blocks[e ^ 1]
        table[e, 2, :2] = (e, e ^ 1)
        table[e, 3, both] = np.arange(owners)
    shard = w_out.shape[1]
    columns = table[:, :2, :chips].reshape(owners, owners, 1) * shard + np.arange(shard)
    numbers = np.zeros((owners, 8, owners * shard), np.int32)
    numbers[:, :4, :owners] = table
    numbers[:, 4] = columns.reshape(owners, -1)
    ids = lax.dynamic_slice(
        jnp.asarray(numbers.reshape(owners * 8, -1)), (8 * me, 0), (8, owners * shard)
    )

    half = rows // 2
    count = width // latent
    gate_up, expert_down = w_gate_up[0, 0], w_expert_down[0, 0]

    def weights_of(x):
        return call(tail_body, (shape((depth, latent), BF), shape((shard, width), BF)), [VMEM])(x)

    def routes_of(x, *others):
        return call(last_body, shape((owners, latent), BF), [VMEM], flops=SHORT, moved=0)(
            after(x, *others)
        )

    def choose(listed, first, second, lines, *others):
        return call(
            functools.partial(choose_body, most),
            (shape((most, width), BF), shape((most + len(lines) * shard, width), BF)),
            [SMEM] + [VMEM] * (3 + len(lines)),
            flops=SHORT,
            moved=0,
        )(ids, after(listed, *others), first, second, *lines)

    def project(own, lines, other):
        parts = [own, *lines, other]
        sizes = ([most] + [shard] * len(lines)) * 2
        results = call(
            functools.partial(gate_up_body, len(parts)),
            tuple(shape((n, gate_up.shape[1]), BF) for n in sizes),
            [VMEM] * (1 + len(parts)),
        )(gate_up, *parts)
        half = len(lines) + 1
        wide.append((results[0], results[half]))
        thin_a.extend(results[1:half])
        thin_b.extend(results[half + 1 :])

    block = half * count
    weights = [
        call(pack_weights_body, shape((depth + shard * count, latent), BF), [VMEM] * 2)(
            w_down_kv[0], w_out[0]
        )
    ]
    weights.append(step(weights[0]))
    small = [weights_of(x) for x in weights]
    second = [
        call(pack_second_body, shape((block + owners, latent), BF), [VMEM] * 4)(
            after(tokens[0], weights[0]),
            routes.transpose(2, 0, 1),
            gates.transpose(2, 0, 1),
            capacity,
        )
    ]
    first = [
        call(pack_first_body, shape((block + depth + shard * count, latent), BF), [VMEM] * 2)(
            after(tokens[0], second[0]), weights[1]
        )
    ]
    listed = [routes_of(second[0])]
    chosen = [choose(listed[0], first[0], second[0], [x[1] for x in small])]
    other = [sibling(chosen[0][1])]
    wide, thin_a, thin_b = [], [], []
    for k in range(1, chips):
        second.append(step(after(second[-1], *[x[0] for x in chosen[k - 2 : k - 1]])))
        passed = first[-1]
        if k == chips - 1:
            passed = call(head_body, shape((block, latent), BF), [VMEM])(passed)
        first.append(step(after(passed, listed[k - 1], *[x[0] for x in wide[k - 2 : k - 1]])))
        listed.append(routes_of(second[k], chosen[k - 1][0]))
        project(
            after(chosen[k - 1][0], listed[k]),
            [x[1] for x in (small[:2] if k == 1 else small[k:])],
            other[k - 1],
        )
        if k < chips - 1:
            small.append(weights_of(first[k]))
            chosen.append(choose(listed[k], first[k], second[k], [small[-1][1]], wide[k - 1][0]))
            other.append(sibling(chosen[k][1]))
    stack = lambda xs: call(stack_body, shape((len(xs), *xs[0].shape), BF), [VMEM] * len(xs))(*xs)
    parts = [stack([x[0] for x in part]) for part in (small[:-1], small[-1:])]
    down = call(unpack_body, shape((owners * depth, latent), BF), [SMEM] + [VMEM] * 4)(
        ids, *parts, *[sibling(x) for x in parts]
    )
    wide_a, wide_b = (stack(thin).reshape(-1, gate_up.shape[1]) for thin in (thin_a, thin_b))

    lat_a, lat_b, groups = [], [], (tuple(range(chips - 1)), (chips - 1,))
    for group in groups:
        lat = call(
            latent_body,
            shape((len(group), rows, latent), BF),
            [VMEM] * (2 + 2 * len(group)),
            flops=0 if lat_a else 2 * SHORT,
            moved=0,
        )(
            after(down, chosen[-1][0], *lat_a),
            kv_gain,
            *[x for k in group for x in (first[k], second[k])],
        )
        lat_a.append(lat)
        lat_b.append(sibling(lat))
    chosen.append(choose(listed[-1], first[-1], second[-1], [], lat_a[1]))
    other.append(sibling(chosen[-1][1]))
    parts = [stack(listed[:-1]), stack(listed[-1:])]
    meta = call(table_body, shape((5 * chips, latent), F32), [SMEM] + [VMEM] * 4)(
        ids, *parts, *[sibling(x) for x in parts]
    )
    att, lat = call(
        functools.partial(attend_body, most, chips, 4, groups),
        (shape((owners * most, latent), BF), shape((owners * rows, latent), BF)),
        [SMEM] + [VMEM] * (3 + 4),
        flops=LONG,
    )(ids, ids, meta, w_query[0], *lat_a, *lat_b)
    out_a = stack([after(x[1], att) for x in small]).reshape(-1, width)
    out_b = sibling(out_a)

    chunks = [(1, 2), (3, 0)] + [(k, k + 1) for k in range(4, chips, 2)]
    mine, theirs = {}, {}

    def expert(ks, *waits):
        picked = [wide[k][side] for side in (0, 1) for k in ks]
        result, away = call(
            functools.partial(expert_body, ks, most, chips),
            (shape((len(ks), most, width), BF),) * 2,
            [VMEM] * (5 + len(picked)),
            flops=LONG // 10,
        )(after(meta, *waits), att, wide_a, wide_b, expert_down, *picked)
        back = sibling(away)
        for i, k in enumerate(ks):
            mine[k], theirs[k] = (result, i), back

    pieces = [(0, width // 2), (width // 2, width - width // 2)]
    passing = [None] * len(pieces)
    expert(chunks[0])
    waiting = list(chunks[1:])
    def combine(k, i, previous, *more):
        start, size = pieces[i]
        return call(
            functools.partial(combine_body, k, mine[k][1], most, chips, start, size),
            shape((rows, size), BF),
            [VMEM] * (3 + len(more)),
            flops=2 * SHORT,
            moved=0,
        )(after(meta, *previous), mine[k][0], theirs[k], *more)

    cross = lambda x: lax.ppermute(x, ("pipe", "expert"), last)
    done = []
    for k in range(1, chips):
        totals = []
        for i in range(len(pieces)):
            more = [] if k == 1 else [passing[i]]
            if i == 0 and chips - 3 <= k < chips - 1:
                more = [after(more[0], kept[k - (chips - 3)])]
            totals.append(combine(k, i, done[-1:], *more))
            done.append(totals[i])
            passing[i] = (cross if k == chips - 1 else step)(totals[i])
        if k == min(2, chips - 2):
            project(after(chosen[-1][0], totals[0]), [], other[-1])
        if waiting and k + 2 >= waiting[0][0]:
            expert(waiting.pop(0), totals[0])
        if k == 3:
            kept = call(
                functools.partial(own_body, mine[0][1], most, chips),
                tuple(shape((rows, size), BF) for _, size in pieces),
                [SMEM] + [VMEM] * 9,
            )(
                ids,
                ids,
                meta,
                w_query[0],
                out_a,
                out_b,
                after(tokens[0], *totals),
                lat,
                mine[0][0],
                theirs[0],
            )
            passing = [after(x, *kept) for x in passing]
            kept = [onward(x) for x in kept]
    output = call(add_body, shape((rows, pieces[0][1]), BF), [VMEM] * 2, flops=2 * SHORT, moved=0)(
        kept[0], passing[0]
    )
    output = call(final_body, shape((rows, width), BF), [VMEM] * 3)(
        output, after(kept[1], output), after(passing[1], output)
    )
    return output[None]


def solution(mesh):
    return jax.shard_map(
        on_device,
        mesh=mesh,
        in_specs=(
            P("pipe", "expert", None),
            P("pipe", "expert", None),
            P("pipe", "expert", None),
            P("pipe", None),
            P("pipe", "expert", None),
            P("pipe", None),
            P("pipe", None, None),
            P("pipe", "expert", None),
            P("pipe", "expert", None, None),
            P("pipe", "expert", None, None),
        ),
        out_specs=P("pipe", "expert", None),
        check_vma=False,
    )
```

```python
import functools

import jax
import jax.numpy as jnp
import numpy as np
from jax import lax
from jax.experimental import pallas as pl
from jax.experimental.pallas import tpu as pltpu
from jax.sharding import PartitionSpec as P

BF = jnp.bfloat16
F32 = jnp.float32
VMEM = pl.BlockSpec(memory_space=pltpu.VMEM)
SMEM = pl.BlockSpec(memory_space=pltpu.SMEM)
MIB = 1024 * 1024
LONG = 10**10
SHORT = 3 * 10**9


def chip_at(place, chips):
    place %= chips
    half = chips // 2
    return 2 * place if place < half else 2 * (chips - 1 - place) + 1


def call(body, outs, ins, limit=8, flops=0, moved=None):
    return pl.pallas_call(
        body,
        out_shape=outs,
        in_specs=ins,
        out_specs=jax.tree.map(lambda _: VMEM, outs),
        compiler_params=pltpu.CompilerParams(vmem_limit_bytes=limit * MIB),
        cost_estimate=pl.CostEstimate(
            flops=flops, transcendentals=0, bytes_accessed=flops // 100 if moved is None else moved
        ),
    )


def dot(a, b):
    return jnp.dot(a, b, preferred_element_type=F32)


def dot_first(a, b):
    return lax.dot_general(a, b, (((0,), (0,)), ((), ())), preferred_element_type=F32)


def dot_last(a, b):
    return lax.dot_general(a, b, (((1,), (1,)), ((), ())), preferred_element_type=F32)


def slots_of(row, most):
    ids = lax.broadcasted_iota(jnp.int32, (most, row.shape[1]), 0).astype(F32)
    return jnp.where(ids == row, 1.0, 0.0)


def blocks_of(x, out, first, latent):
    size = x.shape[0]
    for j in range(x.shape[1] // latent):
        out[first + j * size : first + (j + 1) * size, :] = x[:, j * latent : (j + 1) * latent]


def joined(piece, first, size, count):
    return jnp.concatenate(
        [piece[first + j * size : first + (j + 1) * size, :] for j in range(count)], 1
    )


def pack_weights_body(down, out, weights):
    weights[0 : down.shape[0], :] = down[...]
    blocks_of(out[...], weights, down.shape[0], down.shape[1])


def pack_first_body(tokens, weights, first):
    latent = weights.shape[1]
    blocks_of(tokens[0 : tokens.shape[0] // 2, :], first, 0, latent)
    first[first.shape[0] - weights.shape[0] :, :] = weights[...]


def head_body(piece, out):
    out[...] = piece[0 : out.shape[0], :]


def last_body(piece, out):
    out[...] = piece[piece.shape[0] - out.shape[0] :, :]


def pack_second_body(tokens, routes, gates, capacity, second):
    top, _, rows = routes.shape
    experts = capacity.shape[1]
    half = rows // 2
    latent = second.shape[1]
    blocks_of(tokens[half:rows, :], second, 0, latent)
    expert = lax.broadcasted_iota(jnp.int32, (experts, rows), 0)
    named = jnp.zeros((experts, rows), F32)
    gate = jnp.zeros((experts, rows), F32)
    for k in range(top):
        hit = routes[k] == expert
        named = named + jnp.where(hit, 1.0, 0.0)
        gate = gate + jnp.where(hit, gates[k], 0.0)
    row = lax.broadcasted_iota(jnp.int32, (rows, rows), 0)
    col = lax.broadcasted_iota(jnp.int32, (rows, rows), 1)
    rank = dot(named.astype(BF), jnp.where(row < col, 1.0, 0.0).astype(BF))
    row = lax.broadcasted_iota(jnp.int32, (experts, experts), 0)
    col = lax.broadcasted_iota(jnp.int32, (experts, experts), 1)
    limit = jnp.sum(jnp.where(row == col, capacity[...].astype(F32), 0.0), 1, keepdims=True)
    kept = (named > 0.5) & (rank < limit)
    start = half * (tokens.shape[1] // latent)
    second[start : start + experts, 0:rows] = jnp.where(kept, rank, -1.0).astype(BF)
    second[start : start + experts, rows : 2 * rows] = jnp.where(kept, gate, 0.0).astype(BF)


def tail_body(piece, down, out):
    count = out.shape[1] // piece.shape[1]
    end = piece.shape[0] - out.shape[0] * count
    down[...] = piece[end - down.shape[0] : end, :]
    out[...] = joined(piece, end, out.shape[0], count)


def stack_body(*refs):
    ins, out = refs[:-1], refs[-1]
    for i, piece in enumerate(ins):
        out[i] = piece[...]


def unpack_body(ids, *refs):
    arrays, down = refs[:-1], refs[-1]
    halves = [ref.at[i] for ref in arrays for i in range(ref.shape[0])]
    chips = len(halves) // 2
    depth = halves[0].shape[0]
    for i, half in enumerate(halves):
        side, k = divmod(i, chips)
        down[pl.ds(pl.multiple_of(ids[side, k] * depth, 16), depth), :] = half[...]


def table_body(ids, *refs):
    arrays, meta = refs[:-1], refs[-1]
    halves = [ref.at[i] for ref in arrays for i in range(ref.shape[0])]
    chips = len(halves) // 2
    row = lax.broadcasted_iota(jnp.int32, halves[0].shape, 0)
    for i, half in enumerate(halves):
        side, k = divmod(i, chips)
        table = half[...].astype(F32)
        own = jnp.sum(jnp.where(row == ids[2, 0], table, 0.0), 0, keepdims=True)
        meta[i : i + 1, :] = own
        meta[pl.ds(3 * chips + ids[side, k], 1), :] = own
        if side == 0:
            meta[2 * chips + k : 2 * chips + k + 1, :] = jnp.sum(
                jnp.where(row == ids[2, 1], table, 0.0), 0, keepdims=True
            )


def whole(one, two, rows, count):
    half = rows // 2
    return jnp.concatenate([joined(one, 0, half, count), joined(two, 0, half, count)], 0)


def choose_body(most, ids, small, one, two, *refs):
    lines, (own, other) = refs[:-2], refs[-2:]
    latent = two.shape[1]
    rows = latent // 2
    table = small[...].astype(F32)
    row = lax.broadcasted_iota(jnp.int32, (small.shape[0], rows), 0)
    picks = []
    for which in (0, 1):
        mine = jnp.where(row == ids[2, which], table[:, 0:rows], 0.0)
        picks.append(slots_of(jnp.sum(mine, 0, keepdims=True), most))
    tokens = whole(one, two, rows, own.shape[1] // latent)
    chosen = dot(jnp.concatenate(picks, 0).astype(BF), tokens)
    own[...] = chosen[:most].astype(BF)
    other[0:most, :] = chosen[most:].astype(BF)
    start = most
    for line in lines:
        other[start : start + line.shape[0], :] = line[...]
        start += line.shape[0]


def gate_up_body(count, gate_up, *refs):
    result = dot(jnp.concatenate([ref[...] for ref in refs[:count]], 0), gate_up[...]).astype(BF)
    start = 0
    for out in refs[count:]:
        out[...] = result[start : start + out.shape[0]]
        start += out.shape[0]


def latent_body(down, gain, *refs):
    pieces, latents = refs[:-1], refs[-1]
    rows, latent = latents.shape[1:]
    for i in range(latents.shape[0]):
        x = whole(pieces[2 * i], pieces[2 * i + 1], rows, down.shape[0] // latent)
        raw = dot(x, down[...])
        scale = lax.rsqrt(jnp.mean(raw * raw, -1, keepdims=True) + 1e-06)
        latents[i] = (raw * scale * gain[...]).astype(BF)


def attend(rows, keys, masks, w_query):
    query = (dot(rows, w_query) * (rows.shape[1] ** -0.5)).astype(BF)
    scores = [dot_last(query, piece) for piece in keys]
    scores = [s if m is None else jnp.where(m, s, -1e30) for s, m in zip(scores, masks, strict=True)]
    peak = functools.reduce(jnp.maximum, [jnp.max(s, -1, keepdims=True) for s in scores])
    weights = [jnp.exp(s - peak) for s in scores]
    total = sum(jnp.sum(w, -1, keepdims=True) for w in weights)
    accum = sum(dot(w.astype(BF), piece) for w, piece in zip(weights, keys, strict=True))
    return (accum / total).astype(BF)


def reorder(attended, order):
    place = lax.broadcasted_iota(jnp.int32, (attended.shape[1], order.shape[1]), 0)
    return dot(attended, jnp.where(place == order[4:5, :], 1.0, 0.0).astype(BF)).astype(BF)


def attend_body(most, chips, counts, packs, ids, order, meta, w_query, *refs):
    latents, (att, lat) = refs[:-2], refs[-2:]
    rows = latents[0].shape[1]
    blocks = 2 * chips
    for side in (0, 1):
        for group, ks in enumerate(packs):
            for i, k in enumerate(ks):
                block = pl.multiple_of(ids[side, k] * rows, rows)
                lat[pl.ds(block, rows), :] = latents[side * len(packs) + group][i]
    token = lax.broadcasted_iota(jnp.int32, (most, rows), 1).astype(F32)
    for first in range(0, blocks, counts):
        latent, place = [], []
        for b in range(first, first + counts):
            pick = slots_of(meta[3 * chips + b : 3 * chips + b + 1, 0:rows], most)
            spot = jnp.sum(pick * token, -1, keepdims=True).astype(jnp.int32)
            place.append(spot + (b - first) * rows)
            latent.append(dot(pick.astype(BF), lat[b * rows : (b + 1) * rows, :]).astype(BF))
        place = jnp.concatenate(place, 0)
        key = lax.broadcasted_iota(jnp.int32, (1, counts * rows), 1)
        keys, masks = [lat[first * rows : (first + counts) * rows, :]], [key <= place]
        if first:
            keys.append(lat[0 : first * rows, :])
            masks.append(None)
        attended = attend(jnp.concatenate(latent, 0), keys, masks, w_query[...])
        attended = reorder(attended, order[...])
        for b in range(first, first + counts):
            at = pl.multiple_of(ids[3, b] * most, most)
            att[pl.ds(at, most), :] = attended[(b - first) * most : (b - first + 1) * most, :]


def expert_body(ks, most, chips, meta, att, wide_a, wide_b, expert_down, *refs):
    chosen, outs = refs[:-2], refs[-2:]
    rows = meta.shape[1] // 2
    hidden_width = expert_down.shape[0]
    shard = wide_a.shape[0]
    attended, gate = [], []
    for side in (0, 1):
        for k in ks:
            at = side * chips + k
            pick = slots_of(meta[at : at + 1, 0:rows], most)
            gate.append(jnp.sum(pick * meta[at : at + 1, rows : 2 * rows], -1, keepdims=True))
            attended.append(att[at * most : (at + 1) * most, :])
    attended = jnp.concatenate(attended, 0)
    both = dot(attended[:, :shard], wide_a[...]) + dot(attended[:, shard:], wide_b[...])
    both = both + jnp.concatenate([ref[...] for ref in chosen], 0).astype(F32)
    inner = (jax.nn.silu(both[:, :hidden_width]) * both[:, hidden_width:]).astype(BF)
    result = (dot(inner, expert_down[...]) * jnp.concatenate(gate, 0)).astype(BF)
    for i in range(2 * len(ks)):
        outs[i // len(ks)][i % len(ks)] = result[i * most : (i + 1) * most]


def spread(k, at, most, chips, meta, mine, theirs, cols):
    rows = meta.shape[1] // 2
    one = slots_of(meta[k : k + 1, 0:rows], most).astype(BF)
    two = slots_of(meta[2 * chips + k : 2 * chips + k + 1, 0:rows], most).astype(BF)
    return dot_first(one, mine[at, :, cols]) + dot_first(two, theirs[at, :, cols])


def combine_body(k, at, most, chips, first, size, meta, mine, theirs, *refs):
    total = spread(k, at, most, chips, meta, mine, theirs, slice(first, first + size))
    if len(refs) > 1:
        total = total + refs[0][...].astype(F32)
    refs[-1][...] = total.astype(BF)


def own_body(at, most, chips, ids, order, meta, w_query, out_a, out_b, tokens, lat, mine, theirs, *outs):
    rows = tokens.shape[0]
    start = pl.multiple_of(ids[0, 0] * rows, rows)
    place = start + lax.broadcasted_iota(jnp.int32, (rows, 1), 0)
    key = lax.broadcasted_iota(jnp.int32, (1, lat.shape[0]), 1)
    attended = attend(lat[pl.ds(start, rows), :], [lat[...]], [key <= place], w_query[...])
    attended = reorder(attended, order[...])
    shard = out_a.shape[0]
    hidden = dot(attended[:, :shard], out_a[...]) + dot(attended[:, shard:], out_b[...])
    hidden = (tokens[...].astype(F32) + hidden).astype(BF).astype(F32)
    first = 0
    for out in outs:
        cols = slice(first, first + out.shape[1])
        total = spread(0, at, most, chips, meta, mine, theirs, cols)
        out[...] = (hidden[:, cols] + total).astype(BF)
        first += out.shape[1]


def add_body(one, two, out):
    out[...] = (one[...].astype(F32) + two[...].astype(F32)).astype(BF)


def final_body(first, one, two, out):
    size = first.shape[1]
    out[:, :size] = first[...]
    out[:, size:] = (one[...].astype(F32) + two[...].astype(F32)).astype(BF)


def after(x, *others):
    return lax.optimization_barrier((x, *others))[0]


def on_device(
    tokens, routes, gates, capacity, w_down_kv, kv_gain, w_query, w_out, w_gate_up, w_expert_down
):
    pipes = lax.axis_size("pipe")
    owners = lax.axis_size("expert")
    chips = owners // 2
    me = lax.axis_index("expert")
    rows, width = tokens.shape[1:]
    top = routes.shape[2]
    latent = w_query.shape[1]
    depth = w_down_kv.shape[1]
    most = max(2, 4 * rows * top // (3 * owners))
    shape = jax.ShapeDtypeStruct

    ring, blocks = [], np.zeros((owners, chips), np.int32)
    for r in range(chips):
        even, odd = 2 * chip_at(r, chips), 2 * chip_at(r, chips) + 1
        ring.append((even, 2 * chip_at(r + 1, chips)))
        ring.append((odd, 2 * chip_at(r - 1, chips) + 1))
        for k in range(chips):
            blocks[even, k] = 2 * chip_at(r - k, chips)
            blocks[odd, k] = 2 * chip_at(r + k, chips) + 1
    step = lambda x: lax.ppermute(x, "expert", ring)
    sibling = lambda x: lax.ppermute(x, "expert", [(i, i ^ 1) for i in range(owners)])
    last = [
        (p * owners + a, ((p + 1) % pipes) * owners + b) for p in range(pipes) for a, b in ring
    ]
    onward = lambda x: lax.ppermute(x, "pipe", [(p, (p + 1) % pipes) for p in range(pipes)])

    table = np.zeros((owners, 4, owners), np.int32)
    for e in range(owners):
        both = np.concatenate([blocks[e], blocks[e ^ 1]])
        table[e, 0, :chips], table[e, 1, :chips] = blocks[e], blocks[e ^ 1]
        table[e, 2, :2] = (e, e ^ 1)
        table[e, 3, both] = np.arange(owners)
    shard = w_out.shape[1]
    columns = table[:, :2, :chips].reshape(owners, owners, 1) * shard + np.arange(shard)
    numbers = np.zeros((owners, 8, owners * shard), np.int32)
    numbers[:, :4, :owners] = table
    numbers[:, 4] = columns.reshape(owners, -1)
    ids = lax.dynamic_slice(
        jnp.asarray(numbers.reshape(owners * 8, -1)), (8 * me, 0), (8, owners * shard)
    )

    half = rows // 2
    count = width // latent
    gate_up, expert_down = w_gate_up[0, 0], w_expert_down[0, 0]

    def weights_of(x):
        return call(tail_body, (shape((depth, latent), BF), shape((shard, width), BF)), [VMEM])(x)

    def routes_of(x, *others):
        return call(last_body, shape((owners, latent), BF), [VMEM], flops=SHORT, moved=0)(
            after(x, *others)
        )

    def choose(listed, first, second, lines, *others):
        return call(
            functools.partial(choose_body, most),
            (shape((most, width), BF), shape((most + len(lines) * shard, width), BF)),
            [SMEM] + [VMEM] * (3 + len(lines)),
            flops=SHORT,
            moved=0,
        )(ids, after(listed, *others), first, second, *lines)

    def project(own, lines, other):
        parts = [own, *lines, other]
        sizes = ([most] + [shard] * len(lines)) * 2
        results = call(
            functools.partial(gate_up_body, len(parts)),
            tuple(shape((n, gate_up.shape[1]), BF) for n in sizes),
            [VMEM] * (1 + len(parts)),
        )(gate_up, *parts)
        half = len(lines) + 1
        wide.append((results[0], results[half]))
        thin_a.extend(results[1:half])
        thin_b.extend(results[half + 1 :])

    block = half * count
    weights = [
        call(pack_weights_body, shape((depth + shard * count, latent), BF), [VMEM] * 2)(
            w_down_kv[0], w_out[0]
        )
    ]
    weights.append(step(weights[0]))
    small = [weights_of(x) for x in weights]
    second = [
        call(pack_second_body, shape((block + owners, latent), BF), [VMEM] * 4)(
            after(tokens[0], weights[0]),
            routes.transpose(2, 0, 1),
            gates.transpose(2, 0, 1),
            capacity,
        )
    ]
    first = [
        call(pack_first_body, shape((block + depth + shard * count, latent), BF), [VMEM] * 2)(
            after(tokens[0], second[0]), weights[1]
        )
    ]
    listed = [routes_of(second[0])]
    chosen = [choose(listed[0], first[0], second[0], [x[1] for x in small])]
    other = [sibling(chosen[0][1])]
    wide, thin_a, thin_b = [], [], []
    for k in range(1, chips):
        second.append(step(after(second[-1], *[x[0] for x in chosen[k - 2 : k - 1]])))
        passed = first[-1]
        if k == chips - 1:
            passed = call(head_body, shape((block, latent), BF), [VMEM])(passed)
        first.append(step(after(passed, listed[k - 1], *[x[0] for x in wide[k - 2 : k - 1]])))
        listed.append(routes_of(second[k], chosen[k - 1][0]))
        project(
            after(chosen[k - 1][0], listed[k]),
            [x[1] for x in (small[:2] if k == 1 else small[k:])],
            other[k - 1],
        )
        if k < chips - 1:
            small.append(weights_of(first[k]))
            chosen.append(choose(listed[k], first[k], second[k], [small[-1][1]], wide[k - 1][0]))
            other.append(sibling(chosen[k][1]))
    stack = lambda xs: call(stack_body, shape((len(xs), *xs[0].shape), BF), [VMEM] * len(xs))(*xs)
    parts = [stack([x[0] for x in part]) for part in (small[:-1], small[-1:])]
    down = call(unpack_body, shape((owners * depth, latent), BF), [SMEM] + [VMEM] * 4)(
        ids, *parts, *[sibling(x) for x in parts]
    )
    wide_a, wide_b = (stack(thin).reshape(-1, gate_up.shape[1]) for thin in (thin_a, thin_b))

    parts = [stack(listed[:-1]), stack(listed[-1:])]
    meta = call(table_body, shape((5 * chips, latent), F32), [SMEM] + [VMEM] * 4)(
        ids, *parts, *[sibling(x) for x in parts]
    )
    lat_a, lat_b, groups = [], [], (tuple(range(chips - 1)), (chips - 1,))
    for group in groups:
        lat = call(
            latent_body,
            shape((len(group), rows, latent), BF),
            [VMEM] * (2 + 2 * len(group)),
            flops=0 if lat_a else 2 * SHORT,
            moved=0,
        )(
            after(down, chosen[-1][0], *lat_a),
            kv_gain,
            *[x for k in group for x in (first[k], second[k])],
        )
        lat_a.append(lat)
        lat_b.append(sibling(lat))
    chosen.append(choose(listed[-1], first[-1], second[-1], [], lat_a[1]))
    other.append(sibling(chosen[-1][1]))
    att, lat = call(
        functools.partial(attend_body, most, chips, 8, groups),
        (shape((owners * most, latent), BF), shape((owners * rows, latent), BF)),
        [SMEM] + [VMEM] * (3 + 4),
        flops=LONG,
    )(ids, ids, meta, w_query[0], *lat_a, *lat_b)
    out_a = stack([after(x[1], att) for x in small]).reshape(-1, width)
    out_b = sibling(out_a)

    chunks = [(1, 2), (3, 0)] + [(k, k + 1) for k in range(4, chips, 2)]
    mine, theirs = {}, {}

    def expert(ks, *waits):
        picked = [wide[k][side] for side in (0, 1) for k in ks]
        result, away = call(
            functools.partial(expert_body, ks, most, chips),
            (shape((len(ks), most, width), BF),) * 2,
            [VMEM] * (5 + len(picked)),
            flops=LONG // 10,
        )(after(meta, *waits), att, wide_a, wide_b, expert_down, *picked)
        back = sibling(away)
        for i, k in enumerate(ks):
            mine[k], theirs[k] = (result, i), back

    pieces = [(0, width // 2), (width // 2, width - width // 2)]
    passing = [None] * len(pieces)
    expert(chunks[0])
    waiting = list(chunks[1:])
    def combine(k, i, previous, *more):
        start, size = pieces[i]
        return call(
            functools.partial(combine_body, k, mine[k][1], most, chips, start, size),
            shape((rows, size), BF),
            [VMEM] * (3 + len(more)),
            flops=2 * SHORT,
            moved=0,
        )(after(meta, *previous), mine[k][0], theirs[k], *more)

    cross = lambda x: lax.ppermute(x, ("pipe", "expert"), last)
    done = []
    for k in range(1, chips):
        totals = []
        for i in range(len(pieces)):
            more = [] if k == 1 else [passing[i]]
            if i == 1 and chips - 3 <= k < chips - 1:
                more = [after(more[0], kept[k - (chips - 3)])]
            totals.append(combine(k, i, done[-1:], *more))
            done.append(totals[i])
            passing[i] = (cross if k == chips - 1 else step)(totals[i])
        if k == min(2, chips - 2):
            project(after(chosen[-1][0], totals[0]), [], other[-1])
        if waiting and k + 2 >= waiting[0][0]:
            expert(waiting.pop(0), totals[0])
        if k == 3:
            kept = call(
                functools.partial(own_body, mine[0][1], most, chips),
                tuple(shape((rows, size), BF) for _, size in pieces),
                [SMEM] + [VMEM] * 9,
            )(
                ids,
                ids,
                meta,
                w_query[0],
                out_a,
                out_b,
                after(tokens[0], *totals),
                lat,
                mine[0][0],
                theirs[0],
            )
            passing = [after(x, *kept) for x in passing]
            kept = [onward(x) for x in kept]
    output = call(add_body, shape((rows, pieces[0][1]), BF), [VMEM] * 2, flops=2 * SHORT, moved=0)(
        kept[0], passing[0]
    )
    output = call(final_body, shape((rows, width), BF), [VMEM] * 3)(
        output, after(kept[1], output), after(passing[1], output)
    )
    return output[None]


def solution(mesh):
    return jax.shard_map(
        on_device,
        mesh=mesh,
        in_specs=(
            P("pipe", "expert", None),
            P("pipe", "expert", None),
            P("pipe", "expert", None),
            P("pipe", None),
            P("pipe", "expert", None),
            P("pipe", None),
            P("pipe", None, None),
            P("pipe", "expert", None),
            P("pipe", "expert", None, None),
            P("pipe", "expert", None, None),
        ),
        out_specs=P("pipe", "expert", None),
        check_vma=False,
    )
```
